512 devices in a mesh: section: 16 (over y_lo, z), seq: 32 (over x, y_hi, core).
Axes of the slice: x: 4, y: 8 (y_hi: 4, y_lo: 2; y = y_hi * 2 + y_lo), z: 8, core: 2. Of those that a mesh axis runs over, the one named last changes fastest.
Arguments:
- codes_fwd: bfloat16 [16, 4096, 512], P('section', 'seq'), may hold values from -0.29882812 to 0.29882812
- saved_stream: bfloat16 [16, 4096, 4096], P('section', 'seq'), may hold values from -0.29882812 to 0.29882812
- grad_codes: bfloat16 [16, 4096, 512], P('section', 'seq'), may hold values from -0.29882812 to 0.29882812
- docs_fwd: int32 [16, 4096], P('section', 'seq'), may hold values from 0 to 1, never falling along the last dimension, each value on 1 to 3584 neighbouring positions
- docs_bwd: int32 [16, 4096], P('section', 'seq'), may hold values from 0 to 1, never falling along the last dimension, each value on 1 to 3584 neighbouring positions
- codec: bfloat16 [4096, 512], P(('section', 'seq')), may hold values from -0.25 to 0.25
- wqkv: bfloat16 [16, 4096, 512], P('section', 'seq'), may hold values from -2 to 2
- wout: bfloat16 [16, 4096, 256], P('section', 'seq'), may hold values from -0.375 to 0.375
- gain_attn: bfloat16 [16, 4096], P('section', 'seq'), may hold values from 0.099609375 to 1.8984375
- gain_code: bfloat16 [16, 4096], P('section', 'seq'), may hold values from 0.099609375 to 1.8984375
Outputs:
- codes_next: bfloat16 [16, 4096, 512], P('section', 'seq')
- grads_next: bfloat16 [16, 4096, 512], P('section', 'seq')
The draws below stay inside these ranges and needn't reach their ends.
Inputs may be any that keep to these rules, and one draw needn't show every extreme that they name: `docs_fwd`: ids never fall along a sequence; each document has at most 3584 tokens. `docs_bwd`: ids never fall along a sequence; each document has at most 3584 tokens.
All inputs are finite; a program needn't handle non-finite values.
Results may differ from the reference program's by a relative error of at most 0.023.
Values may be sent and summed in bfloat16 or wider, within the bound.
A program may use at most 128 MiB of HBM per device.

```python
import math
import jax
import jax.numpy as jnp
import numpy as np
from jax import lax

D = 4096
R = 512
HD = 128
HQ = 2
TOK_DEV = 128
SEQ = 4096
N_SECTION = 16
N_SEQ = 32


def draw_wqkv(key, part):
    key = jax.random.fold_in(key, 11)
    first = jax.random.fold_in(key, 0)
    base = jax.random.normal(first, (N_SECTION, D, (HQ + 2) * HD), jnp.float32) * D ** (-0.5)
    return base.astype(jnp.bfloat16)


def levels(own_key, shape, pieces, least, largest):
    factor_of, own = 1.0, jax.random.fold_in(own_key, 6)
    for position, blocks in pieces:
        heights = jnp.exp(jax.random.uniform(jax.random.fold_in(own, position), (blocks,), jnp.float32, least / len(pieces), largest / len(pieces)))
        factor_of = factor_of * jnp.repeat(heights, shape[position] // blocks).reshape([-1 if axis == position else 1 for axis in range(len(shape))])
    return factor_of


def profile(count, total, limit, lean):
    portions = [(1 << 20) // math.isqrt(grade ** lean) + 1 for grade in range(2, count + 1)]
    spare, counts = total - limit - (count - 1), [1] * (count - 1)
    while spare > 0:
        movable = [i for i in range(count - 1) if counts[i] < limit]
        whole, budget = sum([portions[i] for i in movable]), spare
        for i in movable:
            more = min(limit - counts[i], max(1, budget * portions[i] // whole), spare)
            counts[i] = counts[i] + more
            spare = spare - more
    return np.array([limit] + counts)


def ragged_sizes(rng, amount, total, reach, slope):
    if amount == 2:
        one = jax.random.randint(rng, (), max(1, total - reach), min(reach, total - 1) + 1)
        return jnp.stack([one, total - one])
    tallies = jnp.asarray(profile(amount, total, reach, slope), jnp.int32)
    couples = (amount - 1) // 2
    donor, receiver = tallies[1:1 + 2 * couples:2], tallies[2:2 + 2 * couples:2]
    slack = jnp.minimum(donor - 1, reach - receiver)
    passed = jax.random.randint(jax.random.fold_in(rng, 1), (couples,), 0, 1 << 20) % (slack + 1)
    tallies = tallies.at[1:1 + 2 * couples:2].set(donor - passed).at[2:2 + 2 * couples:2].set(receiver + passed)
    return tallies[jax.random.permutation(jax.random.fold_in(rng, 2), amount)]


def normal_values(stream_key, shape, deviation, most, cuts=(), kind=jnp.bfloat16):
    array = deviation * jax.random.normal(stream_key, shape, jnp.float32)
    if cuts:
        array = array * levels(stream_key, shape, cuts, -0.22, 0.18)
    return jnp.clip(array, -most, most).astype(kind)


def setup_inputs(seed: int = 0) -> dict:
    arg_keys = jax.random.split(jax.random.key(seed), 11)
    codes_fwd = normal_values(arg_keys[0], (N_SECTION, SEQ, R), 0.05, 0.29882812, ((0, 16), (1, 32)))
    saved_stream = normal_values(arg_keys[1], (N_SECTION, SEQ, D), 0.05, 0.29882812, ((0, 16), (1, 32)))
    grad_codes = normal_values(arg_keys[2], (N_SECTION, SEQ, R), 0.05, 0.29882812, ((0, 16), (1, 32)))
    docs_fwd = jax.vmap(lambda own: jnp.searchsorted(jnp.cumsum(ragged_sizes(own, 2, SEQ, SEQ * 7 // 8, 0)), jnp.arange(SEQ), side="right"))(jax.random.split(arg_keys[3], N_SECTION)).reshape((N_SECTION, SEQ)).astype(jnp.int32)
    docs_bwd = jax.vmap(lambda own: jnp.searchsorted(jnp.cumsum(ragged_sizes(own, 2, SEQ, SEQ * 7 // 8, 0)), jnp.arange(SEQ), side="right"))(jax.random.split(arg_keys[4], N_SECTION)).reshape((N_SECTION, SEQ)).astype(jnp.int32)
    codec = normal_values(arg_keys[5], (D, R), R ** -0.5, 0.25, ((0, 512),))
    wqkv = draw_wqkv(jax.random.fold_in(arg_keys[10], 71), 0)
    wout = normal_values(arg_keys[7], (N_SECTION, D, HQ * HD), (HQ * HD) ** -0.5, 0.375, ((0, 16), (1, 32)))
    gain_attn = jnp.clip(1.0 + 0.18 * jax.random.normal(arg_keys[8], (N_SECTION, D), jnp.float32), 0.099609375, 1.8984375).astype(jnp.bfloat16)
    gain_code = jnp.clip(1.0 + 0.18 * jax.random.normal(arg_keys[9], (N_SECTION, D), jnp.float32), 0.099609375, 1.8984375).astype(jnp.bfloat16)
    return {"codes_fwd": codes_fwd, "saved_stream": saved_stream, "grad_codes": grad_codes, "docs_fwd": docs_fwd, "docs_bwd": docs_bwd, "codec": codec, "wqkv": wqkv, "wout": wout, "gain_attn": gain_attn, "gain_code": gain_code}


EPS = 1e-05

def rms_factor(values):
    return lax.rsqrt(lax.optimization_barrier(jnp.mean(values * values, axis=-1, keepdims=True)) + EPS)

def make_mask(q_pos, q_docs, k_docs):
    k_pos = jnp.arange(k_docs.shape[0], dtype=jnp.int32)
    return (k_pos[None, :] <= q_pos[:, None]) & (k_docs[None, :] == q_docs[:, None])

def attend_block(queries, q_pos, q_docs, keys, values, k_docs):
    scale = HD ** (-0.5)
    allowed = make_mask(q_pos, q_docs, k_docs)[None]
    scores = jnp.einsum('thd,sd->hts', queries.astype(jnp.float32), keys.astype(jnp.float32)) * scale
    masked = jnp.where(allowed, scores, -1e+30)
    top = lax.optimization_barrier(jnp.max(masked, axis=-1, keepdims=True))
    probs = jnp.where(allowed, jnp.exp(masked - top), 0.0)
    denom = lax.optimization_barrier(jnp.sum(probs, axis=-1, keepdims=True))
    summed = jnp.einsum('hts,sd->htd', probs.astype(jnp.bfloat16).astype(jnp.float32), values.astype(jnp.float32))
    attended = (summed / denom).transpose(1, 0, 2).reshape(queries.shape[0], HQ * HD).astype(jnp.bfloat16)
    return (attended, probs / denom)

def project(stream, wqkv, gain_attn):
    normed = (stream * rms_factor(stream) * gain_attn).astype(jnp.bfloat16)
    qkv = jnp.dot(normed, wqkv, preferred_element_type=jnp.float32).astype(jnp.bfloat16)
    queries = qkv[:, :HQ * HD].reshape(SEQ, HQ, HD)
    keys = qkv[:, HQ * HD:HQ * HD + HD]
    values = qkv[:, HQ * HD + HD:]
    return (queries, keys, values)

def all_attended(queries, keys, values, docs):

    def one_block(index):
        start = (index * TOK_DEV).astype(jnp.int32)
        block_q = lax.dynamic_slice_in_dim(queries, start, TOK_DEV, 0)
        block_docs = lax.dynamic_slice_in_dim(docs, start, TOK_DEV, 0)
        q_pos = start + jnp.arange(TOK_DEV, dtype=jnp.int32)
        return attend_block(block_q, q_pos, block_docs, keys, values, docs)[0]
    return lax.map(one_block, jnp.arange(N_SEQ, dtype=jnp.int32)).reshape(SEQ, HQ * HD)

def forward_section(codes, docs, codec, wqkv, wout, gain_attn, gain_code):
    stream = jnp.dot(codes, codec.T, preferred_element_type=jnp.float32)
    queries, keys, values = project(stream, wqkv, gain_attn)
    attended = all_attended(queries, keys, values, docs)
    mixed = stream + jnp.dot(attended, wout.T, preferred_element_type=jnp.float32)
    normed = (mixed * rms_factor(mixed) * gain_code).astype(jnp.bfloat16)
    coded = jnp.dot(normed, codec, preferred_element_type=jnp.float32) * (R / D) ** 0.5
    return coded.astype(jnp.bfloat16)

def backward_section(saved, grads, docs, codec, wqkv, wout, gain_attn, gain_code):
    stream = saved.astype(jnp.float32)
    scale1 = rms_factor(stream)
    queries, keys, values = project(stream, wqkv, gain_attn)
    attended = all_attended(queries, keys, values, docs)
    mixed = stream + jnp.dot(attended, wout.T, preferred_element_type=jnp.float32)
    scale2 = rms_factor(mixed)
    pre2 = mixed * scale2
    grad_n2 = jnp.dot(grads, codec.T, preferred_element_type=jnp.float32) * (R / D) ** 0.5
    weighted2 = grad_n2 * gain_code
    grad_mixed = scale2 * (weighted2 - pre2 * lax.optimization_barrier(jnp.mean(weighted2 * pre2, axis=-1, keepdims=True)))
    grad_att = jnp.dot(grad_mixed.astype(jnp.bfloat16), wout, preferred_element_type=jnp.float32).astype(jnp.bfloat16)
    scale = HD ** (-0.5)

    def one_block(carry, index):
        start = (index * TOK_DEV).astype(jnp.int32)
        block_q = lax.dynamic_slice_in_dim(queries, start, TOK_DEV, 0)
        block_docs = lax.dynamic_slice_in_dim(docs, start, TOK_DEV, 0)
        block_att = lax.dynamic_slice_in_dim(attended, start, TOK_DEV, 0)
        block_grad = lax.dynamic_slice_in_dim(grad_att, start, TOK_DEV, 0).reshape(TOK_DEV, HQ, HD)
        q_pos = start + jnp.arange(TOK_DEV, dtype=jnp.int32)
        probs = attend_block(block_q, q_pos, block_docs, keys, values, docs)[1]
        grad_f = block_grad.astype(jnp.float32)
        grad_p = jnp.einsum('thd,sd->hts', grad_f, values.astype(jnp.float32))
        delta = jnp.einsum('thd,thd->ht', grad_f, block_att.reshape(TOK_DEV, HQ, HD).astype(jnp.float32))
        grad_s = (probs * (grad_p - delta[..., None]) * scale).astype(jnp.bfloat16).astype(jnp.float32)
        probs_b = probs.astype(jnp.bfloat16).astype(jnp.float32)
        grad_q = jnp.einsum('hts,sd->thd', grad_s, keys.astype(jnp.float32)).reshape(TOK_DEV, HQ * HD)
        key_term = jnp.einsum('hts,thd->sd', grad_s, block_q.astype(jnp.float32))
        value_term = jnp.einsum('hts,thd->sd', probs_b, grad_f)
        key_sum = carry[0] + key_term.astype(jnp.bfloat16).astype(jnp.float32)
        value_sum = carry[1] + value_term.astype(jnp.bfloat16).astype(jnp.float32)
        return ((key_sum, value_sum), grad_q)
    zeros = jnp.zeros((SEQ, HD), jnp.float32)
    sums, grad_q = lax.scan(one_block, (zeros, zeros), jnp.arange(N_SEQ, dtype=jnp.int32))
    grad_q = grad_q.reshape(SEQ, HQ * HD)
    grad_qkv = jnp.concatenate([grad_q, sums[0], sums[1]], axis=1).astype(jnp.bfloat16)
    grad_n1 = jnp.dot(grad_qkv, wqkv.T, preferred_element_type=jnp.float32)
    pre1 = stream * scale1
    weighted1 = grad_n1 * gain_attn
    grad_stream = grad_mixed + scale1 * (weighted1 - pre1 * lax.optimization_barrier(jnp.mean(weighted1 * pre1, axis=-1, keepdims=True)))
    grad_in = jnp.dot(grad_stream.astype(jnp.bfloat16), codec, preferred_element_type=jnp.float32)
    return grad_in.astype(jnp.bfloat16)

def reference(codes_fwd, saved_stream, grad_codes, docs_fwd, docs_bwd, codec, wqkv, wout, gain_attn, gain_code):

    def run_forward(items):
        codes, docs, w_proj, w_back, g_one, g_two = items
        return forward_section(codes, docs, codec, w_proj, w_back, g_one, g_two)

    def run_backward(items):
        saved, grads, docs, w_proj, w_back, g_one, g_two = items
        return backward_section(saved, grads, docs, codec, w_proj, w_back, g_one, g_two)
    sent = lax.map(run_forward, (codes_fwd, docs_fwd, wqkv, wout, gain_attn, gain_code))
    grad_in = lax.map(run_backward, (saved_stream, grad_codes, docs_bwd, wqkv, wout, gain_attn, gain_code))
    return (jnp.roll(sent, 1, axis=0), jnp.roll(grad_in, -1, axis=0))
```

```python
import functools

import jax
import jax.numpy as jnp
from jax import lax
from jax.experimental import pallas as pl
from jax.experimental.pallas import tpu as pltpu
from jax.sharding import PartitionSpec as P

D = 4096
R = 512
HD = 128
HQ = 2
TOK = 128
QKV = (HQ + 2) * HD
QW = HQ * HD
WCAT = QKV + QW
NX, NYH, NC = 4, 4, 2
NYL, NZ = 2, 8
NSEQ = NX * NYH * NC

EPS = 1e-05


class Place:
    def __init__(self):
        self.section = lax.axis_index("section")
        self.seq = lax.axis_index("seq")
        self.ylo = self.section // NZ
        self.z = lax.rem(self.section, NZ)
        self.x = self.seq // (NYH * NC)
        self.yh = lax.rem(self.seq // NC, NYH)
        self.c = lax.rem(self.seq, NC)

    def slot(self, dx=0, dy=0, dc=0):
        x = lax.rem(self.x + (dx + NX), NX)
        yh = lax.rem(self.yh + (dy + NYH), NYH)
        c = lax.rem(self.c + dc, NC)
        return (x * NYH + yh) * NC + c

    def chip(self, dx=0, dy=0):
        return lax.rem(self.x + (dx + NX), NX) * NYH + lax.rem(self.yh + (dy + NYH), NYH)

    def device(self, dx=0, dy=0, dc=0, dz=0, dyl=0):
        z = lax.rem(self.z + (dz + NZ), NZ)
        ylo = lax.rem(self.ylo + dyl, NYL)
        return {"section": ylo * NZ + z, "seq": self.slot(dx, dy, dc)}


class Wire:
    def __init__(self, send_sems, recv_sems):
        self.send_sems, self.recv_sems = send_sems, recv_sems
        self.started = []

    def send(self, src, dst, device):
        k = len(self.started)
        copy = pltpu.make_async_remote_copy(
            src_ref=src,
            dst_ref=dst,
            send_sem=self.send_sems.at[k],
            recv_sem=self.recv_sems.at[k],
            device_id=device,
            device_id_type=pl.DeviceIdType.MESH,
        )
        copy.start()
        self.started.append(copy)
        return k

    def arrived(self, k, dst):
        pltpu.make_async_copy(dst, dst, self.recv_sems.at[k]).wait()

    def finish(self):
        for copy in self.started:
            copy.wait_send()


def meet(devices):
    barrier = pltpu.get_barrier_semaphore()
    for device in devices:
        pl.semaphore_signal(barrier, inc=1, device_id=device, device_id_type=pl.DeviceIdType.MESH)
    pl.semaphore_wait(barrier, len(devices))


class SectionGather:
    def __init__(self, me, wire, out, rows):
        self.me, self.wire, self.out = me, wire, out
        self.half = rows // 2
        self.sib = []
        self.keys = {}

    def block(self, dx, dy):
        return self.out.at[self.me.slot(dx, dy)]

    def part(self, dx, dy, which):
        return self.out.at[self.me.slot(dx, dy), pl.ds(which * self.half, self.half)]

    def to_sibling(self, dx, dy):
        ref = self.block(dx, dy)
        k = self.wire.send(ref, ref, self.me.device(dc=1))
        self.sib.append((k, dx, dy))

    def begin(self):
        own = self.block(0, 0)
        self.keys["y+"] = self.wire.send(own, own, self.me.device(dy=1))
        self.keys["y-"] = self.wire.send(own, own, self.me.device(dy=-1))
        self.along_x(0)
        self.to_sibling(0, 0)

    def along_x(self, dy):
        ref = self.block(0, dy)
        self.keys["x+", dy] = self.wire.send(ref, ref, self.me.device(dx=1))
        self.keys["x-", dy] = self.wire.send(ref, ref, self.me.device(dx=-1))

    def y_near(self):
        self.wire.arrived(self.keys["y+"], self.block(0, -1))
        ref = self.part(0, -1, 0)
        self.keys["y++"] = self.wire.send(ref, ref, self.me.device(dy=1))
        self.along_x(-1)
        self.wire.arrived(self.keys["y-"], self.block(0, 1))
        ref = self.part(0, 1, 1)
        self.keys["y--"] = self.wire.send(ref, ref, self.me.device(dy=-1))
        self.along_x(1)
        self.to_sibling(0, -1)
        self.to_sibling(0, 1)

    def y_far(self):
        self.wire.arrived(self.keys["y++"], self.part(0, 2, 0))
        self.wire.arrived(self.keys["y--"], self.part(0, 2, 1))
        self.along_x(2)
        self.to_sibling(0, 2)

    def x_near(self, dy):
        self.wire.arrived(self.keys["x+", dy], self.block(-1, dy))
        ref = self.part(-1, dy, 0)
        self.keys["x++", dy] = self.wire.send(ref, ref, self.me.device(dx=1))
        self.wire.arrived(self.keys["x-", dy], self.block(1, dy))
        ref = self.part(1, dy, 1)
        self.keys["x--", dy] = self.wire.send(ref, ref, self.me.device(dx=-1))
        self.to_sibling(-1, dy)
        self.to_sibling(1, dy)

    def x_far(self, dy):
        self.wire.arrived(self.keys["x++", dy], self.part(2, dy, 0))
        self.wire.arrived(self.keys["x--", dy], self.part(2, dy, 1))
        self.to_sibling(2, dy)

    def end(self):
        for k, dx, dy in self.sib:
            self.wire.arrived(k, self.out.at[self.me.slot(dx, dy, 1)])

    def partners(self):
        me = self.me
        return [
            me.device(dy=1),
            me.device(dy=-1),
            me.device(dx=1),
            me.device(dx=-1),
            me.device(dc=1),
        ]


CROWS = 16
PLANE = NX * NYH * CROWS
LANES = R // NC


class CodecGather:
    def __init__(self, me, wire, out, both, other, tile):
        self.me, self.wire, self.out = me, wire, out
        self.both, self.other, self.tile = both, other, tile

    def ref(self, first, rows, dc=0):
        c = lax.rem(self.me.c + dc, NC)
        return self.out.at[
            pl.ds(pl.multiple_of(first, CROWS), rows),
            pl.ds(pl.multiple_of(c * LANES, LANES), LANES),
        ]

    def plane_first(self, dyl, dz):
        me = self.me
        ylo = lax.rem(me.ylo + dyl, NYL)
        return (ylo * NZ + lax.rem(me.z + (dz + NZ), NZ)) * PLANE

    def tile_ref(self, dyl, dy):
        return self.ref(self.plane_first(dyl, 0) + self.me.chip(0, dy) * CROWS, CROWS)

    def column_ref(self, dyl, dx):
        x = lax.rem(self.me.x + (dx + NX), NX)
        return self.ref(self.plane_first(dyl, 0) + x * (NYH * CROWS), NYH * CROWS)

    def plane_ref(self, dyl, dz, dc=0):
        return self.ref(self.plane_first(dyl, dz), PLANE, dc)

    def begin(self):
        self.k_pair = self.wire.send(self.both, self.other, self.me.device(dc=1))

    def pair(self, local_sem):
        me = self.me
        self.wire.arrived(self.k_pair, self.other)
        row = lax.broadcasted_iota(jnp.int32, (CROWS, R), 0)
        mine = (row // (CROWS // NC)) == me.c
        self.tile[...] = jnp.where(
            mine, self.both[...].astype(jnp.float32), self.other[...].astype(jnp.float32)
        ).astype(jnp.bfloat16)
        src = self.tile.at[:, pl.ds(pl.multiple_of(me.c * LANES, LANES), LANES)]
        self.local = pltpu.make_async_copy(src, self.tile_ref(0, 0), local_sem)
        self.local.start()
        self.k_y = []
        for dyl in range(NYL):
            for dy in range(NYH):
                if dyl or dy:
                    k = self.wire.send(src, self.tile_ref(0, 0), me.device(dy=dy, dyl=dyl))
                    self.k_y.append((k, dyl, dy))

    def columns(self):
        me = self.me
        self.local.wait()
        for k, dyl, dy in self.k_y:
            self.wire.arrived(k, self.tile_ref(dyl, -dy))
        self.k_x = []
        for dx in (1, -1, 2):
            for dyl in range(NYL):
                ref = self.column_ref(dyl, 0)
                self.k_x.append((self.wire.send(ref, ref, me.device(dx=dx)), dyl, dx))

    def planes(self):
        for k, dyl, dx in self.k_x:
            self.wire.arrived(k, self.column_ref(dyl, -dx))
        self.k_up, self.k_down, self.sib = {}, {}, []
        for dyl in range(NYL):
            self.pass_on(dyl, 0)

    def pass_on(self, dyl, step):
        me = self.me
        below, above = self.plane_ref(dyl, -step), self.plane_ref(dyl, step)
        if step < NZ // 2 - 1 or (step == NZ // 2 - 1 and dyl == 0):
            self.k_up[dyl, step] = self.wire.send(below, below, me.device(dz=1))
        if step < NZ // 2 - 1 or (step == NZ // 2 - 1 and dyl == 1):
            self.k_down[dyl, step] = self.wire.send(above, above, me.device(dz=-1))
        self.to_sibling(dyl, -step)
        if step:
            self.to_sibling(dyl, step)

    def to_sibling(self, dyl, dz):
        ref = self.plane_ref(dyl, dz)
        self.sib.append((self.wire.send(ref, ref, self.me.device(dc=1)), dyl, dz))

    def step(self, step):
        for dyl in range(NYL):
            if step < NZ // 2:
                self.wire.arrived(self.k_up[dyl, step - 1], self.plane_ref(dyl, -step))
                self.wire.arrived(self.k_down[dyl, step - 1], self.plane_ref(dyl, step))
                self.pass_on(dyl, step)
            else:
                keys = self.k_up if dyl == 0 else self.k_down
                self.wire.arrived(keys[dyl, step - 1], self.plane_ref(dyl, step))
                self.to_sibling(dyl, step)

    def end(self):
        for k, dyl, dz in self.sib:
            self.wire.arrived(k, self.plane_ref(dyl, dz, 1))

    def partners(self):
        me = self.me
        return [
            me.device(dy=2),
            me.device(dx=2),
            me.device(dz=1),
            me.device(dz=-1),
        ] + [me.device(dyl=1, dy=dy) for dy in range(NYH)]


def weights_kernel(
    codec_ref, wqkv_ref, wout_ref, docs_f_ref, docs_b_ref, g1_ref, g2_ref,
    codec_out, w_out, meta_out,
    both, other, tile, meta, send_sems, recv_sems, local_sems,
):
    me = Place()
    wire = Wire(send_sems, recv_sems)
    weights = SectionGather(me, wire, w_out, TOK)
    codec = CodecGather(me, wire, codec_out, both, other, tile)
    own = me.slot()
    fills = [
        pltpu.make_async_copy(wqkv_ref.at[0], w_out.at[own, :, pl.ds(0, QKV)], local_sems.at[0]),
        pltpu.make_async_copy(wout_ref.at[0], w_out.at[own, :, pl.ds(QKV, QW)], local_sems.at[1]),
    ]
    for fill in fills:
        fill.start()
    rows = codec_ref[...].astype(jnp.float32)
    both[...] = jnp.concatenate([rows, rows], axis=0).astype(jnp.bfloat16)
    meta[...] = jnp.zeros_like(meta)
    meta[0:1, :] = docs_f_ref[...].astype(jnp.float32)
    meta[1:2, :] = docs_b_ref[...].astype(jnp.float32)
    meta[2:3, :] = g1_ref[...].astype(jnp.float32)
    meta[3:4, :] = g2_ref[...].astype(jnp.float32)
    fill = pltpu.make_async_copy(meta, meta_out.at[me.c, me.chip()], local_sems.at[2])
    fill.start()
    meet(weights.partners() + codec.partners())
    codec.begin()
    for copy in fills:
        copy.wait()
    weights.begin()
    fill.wait()

    def meta_column(dx):
        x = lax.rem(me.x + (dx + NX), NX)
        return meta_out.at[me.c, pl.ds(x * NYH, NYH)]

    m_y = []
    for dy in (1, -1, 2):
        ref = meta_out.at[me.c, me.chip()]
        m_y.append((wire.send(ref, ref, me.device(dy=dy)), dy))
    codec.pair(local_sems.at[3])
    for k, dy in m_y:
        wire.arrived(k, meta_out.at[me.c, me.chip(0, -dy)])
    m_x = []
    for dx in (1, -1, 2):
        ref = meta_column(0)
        m_x.append((wire.send(ref, ref, me.device(dx=dx)), dx))
    codec.columns()
    weights.y_near()
    codec.planes()
    for k, dx in m_x:
        wire.arrived(k, meta_column(-dx))
    ref = meta_out.at[me.c]
    m_s = wire.send(ref, ref, me.device(dc=1))
    weights.x_near(0)
    weights.y_far()
    codec.step(1)
    weights.x_near(-1)
    codec.step(2)
    weights.x_near(1)
    codec.step(3)
    weights.x_near(2)
    for dy in (0, -1, 1, 2):
        weights.x_far(dy)
    codec.step(4)
    wire.arrived(m_s, meta_out.at[1 - me.c])
    weights.end()
    codec.end()
    wire.finish()


ANY = pl.BlockSpec(memory_space=pl.ANY)
VMEM = pl.BlockSpec(memory_space=pltpu.VMEM)


def gather_weights(codec, wqkv, wout, docs_f, docs_b, g1, g2):
    copies = 96
    return pl.pallas_call(
        weights_kernel,
        out_shape=(
            jax.ShapeDtypeStruct((D, R), jnp.bfloat16),
            jax.ShapeDtypeStruct((NSEQ, TOK, WCAT), jnp.bfloat16),
            jax.ShapeDtypeStruct((NC, NX * NYH, 8, TOK), jnp.float32),
        ),
        in_specs=[VMEM, ANY, ANY, VMEM, VMEM, VMEM, VMEM],
        out_specs=(ANY, ANY, ANY),
        scratch_shapes=[
            pltpu.VMEM((CROWS, R), jnp.bfloat16),
            pltpu.VMEM((CROWS, R), jnp.bfloat16),
            pltpu.VMEM((CROWS, R), jnp.bfloat16),
            pltpu.VMEM((8, TOK), jnp.float32),
            pltpu.SemaphoreType.DMA((copies,)),
            pltpu.SemaphoreType.DMA((copies,)),
            pltpu.SemaphoreType.DMA((4,)),
        ],
        compiler_params=pltpu.CompilerParams(collective_id=0, has_side_effects=True),
        name="gather_weights",
    )(codec, wqkv, wout, docs_f, docs_b, g1, g2)


def tokens_kernel(own_ref, out, send_sems, recv_sems, local_sem):
    me = Place()
    wire = Wire(send_sems, recv_sems)
    gather = SectionGather(me, wire, out, TOK)
    fill = pltpu.make_async_copy(own_ref, out.at[me.slot()], local_sem)
    fill.start()
    meet(gather.partners())
    fill.wait()
    gather.begin()
    gather.y_near()
    gather.x_near(0)
    gather.y_far()
    gather.x_near(-1)
    gather.x_near(1)
    gather.x_near(2)
    for dy in (0, -1, 1, 2):
        gather.x_far(dy)
    gather.end()
    wire.finish()


def gather_tokens(own):
    copies = 40
    return pl.pallas_call(
        tokens_kernel,
        out_shape=jax.ShapeDtypeStruct((NSEQ,) + own.shape, own.dtype),
        in_specs=[ANY],
        out_specs=ANY,
        scratch_shapes=[
            pltpu.SemaphoreType.DMA((copies,)),
            pltpu.SemaphoreType.DMA((copies,)),
            pltpu.SemaphoreType.DMA,
        ],
        compiler_params=pltpu.CompilerParams(collective_id=1, has_side_effects=True),
        name="gather_tokens",
    )(own)


def add_into(dst, *others):
    total = dst[...].astype(jnp.float32)
    for other in others:
        total = total + other[...].astype(jnp.float32)
    dst[...] = total.astype(dst.dtype)


def scatter_kernel(
    terms, out, pair, part, far_up, far_down, near_up, near_down, row,
    yfar_up, yfar_down, ynear_up, ynear_down, send_sems, recv_sems,
):
    me = Place()
    wire = Wire(send_sems, recv_sems)
    gather = SectionGather(me, wire, None, TOK)
    meet(gather.partners())
    k = wire.send(terms.at[:, 1 - me.c], pair, me.device(dc=1))
    wire.arrived(k, pair)

    @pl.loop(0, NX * NYH)
    def _(i):
        part[i] = (
            terms[i, me.c].astype(jnp.float32) + pair[i].astype(jnp.float32)
        ).astype(jnp.bfloat16)

    def at_x(dx):
        return lax.rem(me.x + (dx + NX), NX) * NYH

    def group(dx, first, count):
        return part.at[pl.ds(at_x(dx) + first, count)]

    half = NYH // 2
    a = wire.send(group(2, 0, half), far_up, me.device(dx=1))
    b = wire.send(group(2, half, half), far_down, me.device(dx=-1))
    c = wire.send(group(1, half, half), near_up.at[pl.ds(half, half)], me.device(dx=1))
    d = wire.send(group(-1, 0, half), near_down.at[pl.ds(0, half)], me.device(dx=-1))
    wire.arrived(a, far_up)
    add_into(group(1, 0, half), far_up)
    e = wire.send(group(1, 0, half), near_up.at[pl.ds(0, half)], me.device(dx=1))
    wire.arrived(b, far_down)
    add_into(group(-1, half, half), far_down)
    f = wire.send(group(-1, half, half), near_down.at[pl.ds(half, half)], me.device(dx=-1))
    wire.arrived(c, near_up.at[pl.ds(half, half)])
    wire.arrived(d, near_down.at[pl.ds(0, half)])
    wire.arrived(e, near_up.at[pl.ds(0, half)])
    wire.arrived(f, near_down.at[pl.ds(half, half)])
    mine = at_x(0)

    @pl.loop(0, NYH)
    def _(i):
        row[i] = (
            part[mine + i].astype(jnp.float32)
            + near_up[i].astype(jnp.float32)
            + near_down[i].astype(jnp.float32)
        ).astype(jnp.bfloat16)

    def at_y(dy):
        return lax.rem(me.yh + (dy + NYH), NYH)

    rows = TOK // 2
    low, high = pl.ds(0, rows), pl.ds(rows, rows)
    a = wire.send(row.at[at_y(2), low], yfar_up, me.device(dy=1))
    b = wire.send(row.at[at_y(2), high], yfar_down, me.device(dy=-1))
    c = wire.send(row.at[at_y(1), high], ynear_up.at[high], me.device(dy=1))
    d = wire.send(row.at[at_y(-1), low], ynear_down.at[low], me.device(dy=-1))
    wire.arrived(a, yfar_up)
    add_into(row.at[at_y(1), low], yfar_up)
    e = wire.send(row.at[at_y(1), low], ynear_up.at[low], me.device(dy=1))
    wire.arrived(b, yfar_down)
    add_into(row.at[at_y(-1), high], yfar_down)
    f = wire.send(row.at[at_y(-1), high], ynear_down.at[high], me.device(dy=-1))
    wire.arrived(c, ynear_up.at[high])
    wire.arrived(d, ynear_down.at[low])
    wire.arrived(e, ynear_up.at[low])
    wire.arrived(f, ynear_down.at[high])
    out[...] = (
        row[at_y(0)].astype(jnp.float32)
        + ynear_up[...].astype(jnp.float32)
        + ynear_down[...].astype(jnp.float32)
    )
    wire.finish()


def scatter_terms(terms):
    copies = 16
    width = terms.shape[-1]
    b16 = jnp.bfloat16
    return pl.pallas_call(
        scatter_kernel,
        out_shape=jax.ShapeDtypeStruct((TOK, width), jnp.float32),
        in_specs=[VMEM],
        out_specs=VMEM,
        scratch_shapes=[
            pltpu.VMEM((NX * NYH, TOK, width), b16),
            pltpu.VMEM((NX * NYH, TOK, width), b16),
            pltpu.VMEM((NYH // 2, TOK, width), b16),
            pltpu.VMEM((NYH // 2, TOK, width), b16),
            pltpu.VMEM((NYH, TOK, width), b16),
            pltpu.VMEM((NYH, TOK, width), b16),
            pltpu.VMEM((NYH, TOK, width), b16),
            pltpu.VMEM((TOK // 2, width), b16),
            pltpu.VMEM((TOK // 2, width), b16),
            pltpu.VMEM((TOK, width), b16),
            pltpu.VMEM((TOK, width), b16),
            pltpu.SemaphoreType.DMA((copies,)),
            pltpu.SemaphoreType.DMA((copies,)),
        ],
        compiler_params=pltpu.CompilerParams(
            collective_id=2, has_side_effects=True, vmem_limit_bytes=32 * 2**20
        ),
        name="scatter_terms",
    )(terms.reshape(NX * NYH, NC, TOK, width))


def shifted(value, axis, steps):
    count = lax.axis_size(axis)
    pairs = [(source, (source + steps) % count) for source in range(count)]
    return lax.ppermute(value, axis, pairs)


def rms_factor(values):
    return lax.rsqrt(jnp.mean(values * values, axis=-1, keepdims=True) + EPS)


def to_heads(matrix, rows):
    return matrix.reshape(rows, HQ, HD).transpose(1, 0, 2)


def from_heads(heads, rows):
    return heads.transpose(1, 0, 2).reshape(rows, HQ * HD)


def on_device(
    codes_fwd, saved_stream, grad_codes, docs_fwd, docs_bwd, codec, wqkv, wout, gain_attn, gain_code
):
    rows = codes_fwd.shape[1]
    scale = HD ** (-0.5)
    enc_scale = (R / D) ** 0.5
    codec_all, w_cat, meta = gather_weights(
        codec, wqkv, wout, docs_fwd, docs_bwd, gain_attn, gain_code
    )
    w_cat = w_cat.reshape(D, WCAT)
    w_all, o_all = w_cat[:, :QKV], w_cat[:, QKV:]
    meta = meta.transpose(2, 1, 0, 3).reshape(8, D)
    all_docs_f, all_docs_b = meta[0:1], meta[1:2]
    g_attn, g_code = meta[2:3], meta[3:4]
    place = lax.axis_index("seq") * rows + jnp.arange(rows, dtype=jnp.int32)
    k_pos = jnp.arange(D, dtype=jnp.int32)
    causal = k_pos[None, :] <= place[:, None]
    contract_last = (((1,), (1,)), ((), ()))

    def project(stream):
        scale1 = rms_factor(stream)
        normed = (stream * scale1 * g_attn).astype(jnp.bfloat16)
        return scale1, jnp.dot(normed, w_all, preferred_element_type=jnp.float32).astype(
            jnp.bfloat16
        )

    def finish_forward(stream, attended):
        return stream + lax.dot_general(
            attended, o_all, contract_last, preferred_element_type=jnp.float32
        )

    def attend(queries, keys, values, docs, all_docs):
        allowed = (causal & (all_docs == docs.astype(jnp.float32)[:, None]))[None]
        scores = (
            jnp.einsum("htd,sd->hts", queries, keys, preferred_element_type=jnp.float32) * scale
        )
        masked = jnp.where(allowed, scores, -1e30)
        top = jnp.max(masked, axis=-1, keepdims=True)
        probs = jnp.where(allowed, jnp.exp(masked - top), 0.0)
        denom = jnp.sum(probs, axis=-1, keepdims=True)
        summed = jnp.einsum(
            "hts,sd->htd", probs.astype(jnp.bfloat16), values, preferred_element_type=jnp.float32
        )
        return probs, denom, (summed / denom).astype(jnp.bfloat16)

    stream = lax.dot_general(
        codes_fwd[0], codec_all, contract_last, preferred_element_type=jnp.float32
    )
    _, qkv = project(stream)
    saved = saved_stream[0].astype(jnp.float32)
    scale1, qkv_b = project(saved)
    kv = gather_tokens(jnp.concatenate([qkv[:, QW:], qkv_b[:, QW:]], axis=1)).reshape(D, QKV)

    _, _, heads = attend(
        to_heads(qkv[:, :QW], rows), kv[:, :HD], kv[:, HD : 2 * HD], docs_fwd[0], all_docs_f
    )
    mixed = finish_forward(stream, from_heads(heads, rows))
    normed = (mixed * rms_factor(mixed) * g_code).astype(jnp.bfloat16)
    coded = (jnp.dot(normed, codec_all, preferred_element_type=jnp.float32) * enc_scale).astype(
        jnp.bfloat16
    )
    codes_out = shifted(coded, "section", 1)

    stream = saved
    queries_b = to_heads(qkv_b[:, :QW], rows)
    all_keys, all_values = kv[:, 2 * HD : 3 * HD], kv[:, 3 * HD :]
    probs, denom, attended_heads = attend(
        queries_b, all_keys, all_values, docs_bwd[0], all_docs_b
    )
    mixed = finish_forward(stream, from_heads(attended_heads, rows))
    scale2 = rms_factor(mixed)
    pre2 = mixed * scale2
    grad_n2 = (
        lax.dot_general(grad_codes[0], codec_all, contract_last, preferred_element_type=jnp.float32)
        * enc_scale
    )
    weighted2 = grad_n2 * g_code
    grad_mixed = scale2 * (weighted2 - pre2 * jnp.mean(weighted2 * pre2, axis=-1, keepdims=True))
    grad_att = jnp.dot(
        grad_mixed.astype(jnp.bfloat16), o_all, preferred_element_type=jnp.float32
    ).astype(jnp.bfloat16)
    grad_heads = to_heads(grad_att, rows)
    grad_p = jnp.einsum("htd,sd->hts", grad_heads, all_values, preferred_element_type=jnp.float32)
    delta = jnp.einsum(
        "htd,htd->ht", grad_heads.astype(jnp.float32), attended_heads.astype(jnp.float32)
    )
    grad_s = (probs / denom * (grad_p - delta[..., None]) * scale).astype(jnp.bfloat16)
    probs_b = (probs / denom).astype(jnp.bfloat16)
    grad_q = from_heads(
        jnp.einsum("hts,sd->htd", grad_s, all_keys, preferred_element_type=jnp.float32), rows
    )
    key_term = jnp.einsum("hts,htd->sd", grad_s, queries_b, preferred_element_type=jnp.float32)
    value_term = jnp.einsum("hts,htd->sd", probs_b, grad_heads, preferred_element_type=jnp.float32)
    kv_grad = scatter_terms(
        jnp.concatenate([key_term, value_term], axis=1).astype(jnp.bfloat16)
    )
    grad_qkv = jnp.concatenate([grad_q, kv_grad], axis=1).astype(jnp.bfloat16)
    grad_n1 = lax.dot_general(grad_qkv, w_all, contract_last, preferred_element_type=jnp.float32)
    pre1 = stream * scale1
    weighted1 = grad_n1 * g_attn
    grad_stream = grad_mixed + scale1 * (
        weighted1 - pre1 * jnp.mean(weighted1 * pre1, axis=-1, keepdims=True)
    )
    grad_in = jnp.dot(
        grad_stream.astype(jnp.bfloat16), codec_all, preferred_element_type=jnp.float32
    ).astype(jnp.bfloat16)
    grads_out = shifted(grad_in, "section", -1)
    return (codes_out[None], grads_out[None])


def solution(mesh):
    return jax.shard_map(
        on_device,
        mesh=mesh,
        in_specs=(
            P("section", "seq", None),
            P("section", "seq", None),
            P("section", "seq", None),
            P("section", "seq"),
            P("section", "seq"),
            P(("section", "seq"), None),
            P("section", "seq", None),
            P("section", "seq", None),
            P("section", "seq"),
            P("section", "seq"),
        ),
        out_specs=(P("section", "seq", None), P("section", "seq", None)),
        check_vma=False,
    )
```

```python
import functools

import jax
import jax.numpy as jnp
from jax import lax
from jax.experimental import pallas as pl
from jax.experimental.pallas import tpu as pltpu
from jax.sharding import PartitionSpec as P

D = 4096
R = 512
HD = 128
HQ = 2
TOK = 128
QKV = (HQ + 2) * HD
QW = HQ * HD
NX, NYH, NC = 4, 4, 2
NYL, NZ = 2, 8
NSEQ = NX * NYH * NC
NG = NX
GW = D // NG
GS = NSEQ // NG
KEYS = 512
KS = KEYS // TOK
NK = D // KEYS

EPS = 1e-05


class Place:
    def __init__(self):
        self.section = lax.axis_index("section")
        self.seq = lax.axis_index("seq")
        self.ylo = self.section // NZ
        self.z = lax.rem(self.section, NZ)
        self.x = self.seq // (NYH * NC)
        self.yh = lax.rem(self.seq // NC, NYH)
        self.c = lax.rem(self.seq, NC)

    def slot(self, dx=0, dy=0, dc=0):
        x = lax.rem(self.x + (dx + NX), NX)
        yh = lax.rem(self.yh + (dy + NYH), NYH)
        c = lax.rem(self.c + dc, NC)
        return (x * NYH + yh) * NC + c

    def chip(self, dx=0, dy=0):
        return lax.rem(self.x + (dx + NX), NX) * NYH + lax.rem(self.yh + (dy + NYH), NYH)

    def device(self, dx=0, dy=0, dc=0, dz=0, dyl=0):
        z = lax.rem(self.z + (dz + NZ), NZ)
        ylo = lax.rem(self.ylo + dyl, NYL)
        return {"section": ylo * NZ + z, "seq": self.slot(dx, dy, dc)}


class Wire:
    def __init__(self, send_sems, recv_sems):
        self.send_sems, self.recv_sems = send_sems, recv_sems
        self.started = []

    def send(self, src, dst, device):
        k = len(self.started)
        copy = pltpu.make_async_remote_copy(
            src_ref=src,
            dst_ref=dst,
            send_sem=self.send_sems.at[k],
            recv_sem=self.recv_sems.at[k],
            device_id=device,
            device_id_type=pl.DeviceIdType.MESH,
        )
        copy.start()
        self.started.append(copy)
        return k

    def arrived(self, k, dst):
        pltpu.make_async_copy(dst, dst, self.recv_sems.at[k]).wait()

    def finish(self):
        for copy in self.started:
            copy.wait_send()


def meet(devices):
    barrier = pltpu.get_barrier_semaphore()
    for device in devices:
        pl.semaphore_signal(barrier, inc=1, device_id=device, device_id_type=pl.DeviceIdType.MESH)
    pl.semaphore_wait(barrier, len(devices))


class SectionGather:
    def __init__(self, me, wire, out, rows):
        self.me, self.wire, self.out = me, wire, out
        self.half = rows // 2
        self.sib = []
        self.keys = {}

    def block(self, dx, dy):
        return self.out.at[self.me.slot(dx, dy)]

    def part(self, dx, dy, which):
        return self.out.at[self.me.slot(dx, dy), pl.ds(which * self.half, self.half)]

    def to_sibling(self, dx, dy):
        ref = self.block(dx, dy)
        k = self.wire.send(ref, ref, self.me.device(dc=1))
        self.sib.append((k, dx, dy))

    def begin(self):
        own = self.block(0, 0)
        self.keys["y+"] = self.wire.send(own, own, self.me.device(dy=1))
        self.keys["y-"] = self.wire.send(own, own, self.me.device(dy=-1))
        self.along_x(0)
        self.to_sibling(0, 0)

    def along_x(self, dy):
        ref = self.block(0, dy)
        self.keys["x+", dy] = self.wire.send(ref, ref, self.me.device(dx=1))
        self.keys["x-", dy] = self.wire.send(ref, ref, self.me.device(dx=-1))

    def y_near(self):
        self.wire.arrived(self.keys["y+"], self.block(0, -1))
        ref = self.part(0, -1, 0)
        self.keys["y++"] = self.wire.send(ref, ref, self.me.device(dy=1))
        self.along_x(-1)
        self.wire.arrived(self.keys["y-"], self.block(0, 1))
        ref = self.part(0, 1, 1)
        self.keys["y--"] = self.wire.send(ref, ref, self.me.device(dy=-1))
        self.along_x(1)
        self.to_sibling(0, -1)
        self.to_sibling(0, 1)

    def y_far(self):
        self.wire.arrived(self.keys["y++"], self.part(0, 2, 0))
        self.wire.arrived(self.keys["y--"], self.part(0, 2, 1))
        self.along_x(2)
        self.to_sibling(0, 2)

    def x_near(self, dy):
        self.wire.arrived(self.keys["x+", dy], self.block(-1, dy))
        ref = self.part(-1, dy, 0)
        self.keys["x++", dy] = self.wire.send(ref, ref, self.me.device(dx=1))
        self.wire.arrived(self.keys["x-", dy], self.block(1, dy))
        ref = self.part(1, dy, 1)
        self.keys["x--", dy] = self.wire.send(ref, ref, self.me.device(dx=-1))
        self.to_sibling(-1, dy)
        self.to_sibling(1, dy)

    def x_far(self, dy):
        self.wire.arrived(self.keys["x++", dy], self.part(2, dy, 0))
        self.wire.arrived(self.keys["x--", dy], self.part(2, dy, 1))
        self.to_sibling(2, dy)

    def end(self):
        for k, dx, dy in self.sib:
            self.wire.arrived(k, self.out.at[self.me.slot(dx, dy, 1)])

    def partners(self):
        me = self.me
        return [
            me.device(dy=1),
            me.device(dy=-1),
            me.device(dx=1),
            me.device(dx=-1),
            me.device(dc=1),
        ]


CROWS = 16
PLANE = NX * NYH * CROWS
LANES = R // NC


class CodecGather:
    def __init__(self, me, wire, out, both, other, tile):
        self.me, self.wire, self.out = me, wire, out
        self.both, self.other, self.tile = both, other, tile

    def ref(self, first, rows, dc=0):
        c = lax.rem(self.me.c + dc, NC)
        return self.out.at[
            pl.ds(pl.multiple_of(first, CROWS), rows),
            pl.ds(pl.multiple_of(c * LANES, LANES), LANES),
        ]

    def plane_first(self, dyl, dz):
        me = self.me
        ylo = lax.rem(me.ylo + dyl, NYL)
        return (ylo * NZ + lax.rem(me.z + (dz + NZ), NZ)) * PLANE

    def tile_ref(self, dyl, dy):
        return self.ref(self.plane_first(dyl, 0) + self.me.chip(0, dy) * CROWS, CROWS)

    def column_ref(self, dyl, dx):
        x = lax.rem(self.me.x + (dx + NX), NX)
        return self.ref(self.plane_first(dyl, 0) + x * (NYH * CROWS), NYH * CROWS)

    def plane_ref(self, dyl, dz, dc=0):
        return self.ref(self.plane_first(dyl, dz), PLANE, dc)

    def begin(self):
        self.k_pair = self.wire.send(self.both, self.other, self.me.device(dc=1))

    def pair(self, local_sem):
        me = self.me
        self.wire.arrived(self.k_pair, self.other)
        row = lax.broadcasted_iota(jnp.int32, (CROWS, R), 0)
        mine = (row // (CROWS // NC)) == me.c
        self.tile[...] = jnp.where(
            mine, self.both[...].astype(jnp.float32), self.other[...].astype(jnp.float32)
        ).astype(jnp.bfloat16)
        src = self.tile.at[:, pl.ds(pl.multiple_of(me.c * LANES, LANES), LANES)]
        self.local = pltpu.make_async_copy(src, self.tile_ref(0, 0), local_sem)
        self.local.start()
        self.k_y = []
        for dyl in range(NYL):
            for dy in range(NYH):
                if dyl or dy:
                    k = self.wire.send(src, self.tile_ref(0, 0), me.device(dy=dy, dyl=dyl))
                    self.k_y.append((k, dyl, dy))

    def columns(self):
        me = self.me
        self.local.wait()
        for k, dyl, dy in self.k_y:
            self.wire.arrived(k, self.tile_ref(dyl, -dy))
        self.k_x = []
        for dx in (1, -1, 2):
            for dyl in range(NYL):
                ref = self.column_ref(dyl, 0)
                self.k_x.append((self.wire.send(ref, ref, me.device(dx=dx)), dyl, dx))

    def planes(self):
        for k, dyl, dx in self.k_x:
            self.wire.arrived(k, self.column_ref(dyl, -dx))
        self.k_up, self.k_down, self.sib = {}, {}, []
        for dyl in range(NYL):
            self.pass_on(dyl, 0)

    def pass_on(self, dyl, step):
        me = self.me
        below, above = self.plane_ref(dyl, -step), self.plane_ref(dyl, step)
        if step < NZ // 2 - 1 or (step == NZ // 2 - 1 and dyl == 0):
            self.k_up[dyl, step] = self.wire.send(below, below, me.device(dz=1))
        if step < NZ // 2 - 1 or (step == NZ // 2 - 1 and dyl == 1):
            self.k_down[dyl, step] = self.wire.send(above, above, me.device(dz=-1))
        self.to_sibling(dyl, -step)
        if step:
            self.to_sibling(dyl, step)

    def to_sibling(self, dyl, dz):
        ref = self.plane_ref(dyl, dz)
        self.sib.append((self.wire.send(ref, ref, self.me.device(dc=1)), dyl, dz))

    def step(self, step):
        for dyl in range(NYL):
            if step < NZ // 2:
                self.wire.arrived(self.k_up[dyl, step - 1], self.plane_ref(dyl, -step))
                self.wire.arrived(self.k_down[dyl, step - 1], self.plane_ref(dyl, step))
                self.pass_on(dyl, step)
            else:
                keys = self.k_up if dyl == 0 else self.k_down
                self.wire.arrived(keys[dyl, step - 1], self.plane_ref(dyl, step))
                self.to_sibling(dyl, step)

    def end(self):
        for k, dyl, dz in self.sib:
            self.wire.arrived(k, self.plane_ref(dyl, dz, 1))

    def partners(self):
        me = self.me
        return [
            me.device(dy=2),
            me.device(dx=2),
            me.device(dz=1),
            me.device(dz=-1),
        ] + [me.device(dyl=1, dy=dy) for dy in range(NYH)]


class MetaGather:
    def __init__(self, me, wire, buf):
        self.me, self.wire, self.buf = me, wire, buf

    def column(self, dx):
        x = lax.rem(self.me.x + (dx + NX), NX)
        return self.buf.at[self.me.c, pl.ds(x * NYH, NYH)]

    def begin(self):
        me, self.k = self.me, []
        for dy in (1, -1, 2):
            ref = self.buf.at[me.c, me.chip()]
            self.k.append((self.wire.send(ref, ref, me.device(dy=dy)), dy))

    def columns(self):
        me = self.me
        for k, dy in self.k:
            self.wire.arrived(k, self.buf.at[me.c, me.chip(0, -dy)])
        self.k = []
        for dx in (1, -1, 2):
            ref = self.column(0)
            self.k.append((self.wire.send(ref, ref, me.device(dx=dx)), dx))

    def pair(self):
        for k, dx in self.k:
            self.wire.arrived(k, self.column(-dx))
        ref = self.buf.at[self.me.c]
        self.k_pair = self.wire.send(ref, ref, self.me.device(dc=1))

    def end(self):
        self.wire.arrived(self.k_pair, self.buf.at[1 - self.me.c])


def add_into(dst, *others):
    total = dst[...].astype(jnp.float32)
    for other in others:
        total = total + other[...].astype(jnp.float32)
    dst[...] = total.astype(dst.dtype)


class TermScatter:
    def __init__(self, me, wire, terms, bufs):
        self.me, self.wire, self.terms = me, wire, terms
        (self.pair, self.part, self.far_up, self.far_down, self.near_up, self.near_down,
         self.row, self.yfar_up, self.yfar_down, self.ynear_up, self.ynear_down) = bufs
        self.k_pair = []

    def send_pair(self, group):
        chips = pl.ds(group * NYH, NYH)
        k = self.wire.send(
            self.terms.at[chips, 1 - self.me.c], self.pair.at[chips], self.me.device(dc=1)
        )
        self.k_pair.append((k, group))

    def at_x(self, dx):
        return lax.rem(self.me.x + (dx + NX), NX) * NYH

    def group(self, dx, first, count):
        return self.part.at[pl.ds(self.at_x(dx) + first, count)]

    def along_x(self):
        me, wire = self.me, self.wire
        for k, group in self.k_pair:
            wire.arrived(k, self.pair.at[pl.ds(group * NYH, NYH)])

        @pl.loop(0, NX * NYH)
        def _(i):
            self.part[i] = (
                self.terms[i, me.c].astype(jnp.float32) + self.pair[i].astype(jnp.float32)
            ).astype(jnp.bfloat16)

        half = NYH // 2
        near_up, near_down = self.near_up, self.near_down
        self.a = wire.send(self.group(2, 0, half), self.far_up, me.device(dx=1))
        self.b = wire.send(self.group(2, half, half), self.far_down, me.device(dx=-1))
        self.c = wire.send(
            self.group(1, half, half), near_up.at[pl.ds(half, half)], me.device(dx=1)
        )
        self.d = wire.send(
            self.group(-1, 0, half), near_down.at[pl.ds(0, half)], me.device(dx=-1)
        )

    def x_far(self):
        me, wire = self.me, self.wire
        half = NYH // 2
        wire.arrived(self.a, self.far_up)
        add_into(self.group(1, 0, half), self.far_up)
        self.e = wire.send(
            self.group(1, 0, half), self.near_up.at[pl.ds(0, half)], me.device(dx=1)
        )
        wire.arrived(self.b, self.far_down)
        add_into(self.group(-1, half, half), self.far_down)
        self.f = wire.send(
            self.group(-1, half, half), self.near_down.at[pl.ds(half, half)], me.device(dx=-1)
        )

    def at_y(self, dy):
        return lax.rem(self.me.yh + (dy + NYH), NYH)

    def along_y(self):
        me, wire = self.me, self.wire
        half = NYH // 2
        wire.arrived(self.c, self.near_up.at[pl.ds(half, half)])
        wire.arrived(self.d, self.near_down.at[pl.ds(0, half)])
        wire.arrived(self.e, self.near_up.at[pl.ds(0, half)])
        wire.arrived(self.f, self.near_down.at[pl.ds(half, half)])
        mine = self.at_x(0)
        row = self.row

        @pl.loop(0, NYH)
        def _(i):
            row[i] = (
                self.part[mine + i].astype(jnp.float32)
                + self.near_up[i].astype(jnp.float32)
                + self.near_down[i].astype(jnp.float32)
            ).astype(jnp.bfloat16)

        rows = TOK // 2
        low, high = pl.ds(0, rows), pl.ds(rows, rows)
        at_y = self.at_y
        self.a = wire.send(row.at[at_y(2), low], self.yfar_up, me.device(dy=1))
        self.b = wire.send(row.at[at_y(2), high], self.yfar_down, me.device(dy=-1))
        self.c = wire.send(row.at[at_y(1), high], self.ynear_up.at[high], me.device(dy=1))
        self.d = wire.send(row.at[at_y(-1), low], self.ynear_down.at[low], me.device(dy=-1))

    def y_far(self):
        me, wire, row, at_y = self.me, self.wire, self.row, self.at_y
        rows = TOK // 2
        low, high = pl.ds(0, rows), pl.ds(rows, rows)
        wire.arrived(self.a, self.yfar_up)
        add_into(row.at[at_y(1), low], self.yfar_up)
        self.e = wire.send(row.at[at_y(1), low], self.ynear_up.at[low], me.device(dy=1))
        wire.arrived(self.b, self.yfar_down)
        add_into(row.at[at_y(-1), high], self.yfar_down)
        self.f = wire.send(row.at[at_y(-1), high], self.ynear_down.at[high], me.device(dy=-1))

    def result(self):
        wire = self.wire
        rows = TOK // 2
        low, high = pl.ds(0, rows), pl.ds(rows, rows)
        wire.arrived(self.c, self.ynear_up.at[high])
        wire.arrived(self.d, self.ynear_down.at[low])
        wire.arrived(self.e, self.ynear_up.at[low])
        wire.arrived(self.f, self.ynear_down.at[high])
        return (
            self.row[self.at_y(0)].astype(jnp.float32)
            + self.ynear_up[...].astype(jnp.float32)
            + self.ynear_down[...].astype(jnp.float32)
        )


def dot(a, b, dims):
    return lax.dot_general(a, b, (dims, ((), ())), preferred_element_type=jnp.float32)


NN = ((1,), (0,))
NT = ((1,), (1,))
TN = ((0,), (0,))
F32, B16 = jnp.float32, jnp.bfloat16
SCALE = HD ** (-0.5)
ENC = (R / D) ** 0.5


def row_sum(values):
    return jnp.sum(values, axis=-1, keepdims=True)


def rms_of(total):
    return lax.rsqrt(total * (1.0 / D) + EPS)


def stack_heads(matrix):
    return jnp.concatenate([matrix[:, h * HD : (h + 1) * HD] for h in range(HQ)], axis=0)


def from_columns(columns):
    return jnp.concatenate(
        [columns[:, h * TOK : (h + 1) * TOK].T for h in range(HQ)], axis=1
    )


def to_columns(matrix):
    return jnp.concatenate([matrix[:, h * HD : (h + 1) * HD].T for h in range(HQ)], axis=1)


def tick_kernel(
    codes_ref, saved_ref, grads_ref, docs_f_ref, docs_b_ref, codec_ref, wqkv_ref, wout_ref,
    g1_ref, g2_ref,
    codes_out, grads_out,
    wq, wo, cd, meta, rows, sv, st, gm, mx, kvf, kvb, probs, terms, sent, gin,
    both, other, tile,
    pair, part, far_up, far_down, near_up, near_down, row, yfar_up, yfar_down, ynear_up, ynear_down,
    send_sems, recv_sems, local_sems,
):
    me = Place()
    wire = Wire(send_sems, recv_sems)
    weights = SectionGather(me, wire, wq, TOK)
    outs = SectionGather(me, wire, wo, TOK)
    codec = CodecGather(me, wire, cd, both, other, tile)
    metas = MetaGather(me, wire, meta)
    back = SectionGather(me, wire, kvb, TOK)
    fore = SectionGather(me, wire, kvf, TOK)
    scatter = TermScatter(
        me, wire, terms,
        (pair, part, far_up, far_down, near_up, near_down, row,
         yfar_up, yfar_down, ynear_up, ynear_down),
    )
    own = me.slot()
    sections = NYL * NZ
    after = {"section": lax.rem(me.section + 1, sections), "seq": me.seq}
    before = {"section": lax.rem(me.section + sections - 1, sections), "seq": me.seq}

    fill_q = pltpu.make_async_copy(wqkv_ref.at[0], wq.at[own], local_sems.at[0])
    fill_o = pltpu.make_async_copy(wout_ref.at[0], wo.at[own], local_sems.at[1])
    fill_s = [
        pltpu.make_async_copy(
            saved_ref.at[:, pl.ds(g * GW, GW)], sv.at[g], local_sems.at[3 + g]
        )
        for g in range(NG)
    ]
    for copy in [fill_q, fill_o] + fill_s:
        copy.start()
    tall = codec_ref[...].astype(F32)
    both[...] = jnp.concatenate([tall, tall], axis=0).astype(B16)
    docs_f, docs_b = docs_f_ref[...].astype(F32), docs_b_ref[...].astype(F32)
    meta[me.c, me.chip()] = jnp.concatenate(
        [docs_f, docs_b, g1_ref[...].astype(F32), g2_ref[...].astype(F32), jnp.zeros((4, TOK), F32)],
        axis=0,
    )
    meet(weights.partners() + codec.partners() + [after, before])
    codec.begin()
    fill_q.wait()
    weights.begin()
    metas.begin()
    fill_o.wait()
    for copy in fill_s:
        copy.wait()

    def square_step(g, total):
        values = sv[g].astype(F32)
        return total + row_sum(values * values)

    zero = jnp.zeros((TOK, 1), F32)
    r1b = rms_of(lax.fori_loop(0, NG, square_step, zero))
    codec.pair(local_sems.at[2])
    metas.columns()
    codec.columns()
    weights.y_near()
    metas.pair()
    codec.planes()
    weights.x_near(0)
    weights.y_far()
    codec.step(1)
    outs.begin()
    weights.x_near(-1)
    codec.step(2)
    weights.x_near(1)
    outs.y_near()
    weights.x_near(2)
    metas.end()
    for q in range(NSEQ):
        rows[q // GS, :, q % GS * TOK : (q % GS + 1) * TOK] = meta[q % NC, q // NC]
    codec.step(3)
    for dy in (0, -1, 1, 2):
        weights.x_far(dy)
    outs.x_near(0)
    outs.y_far()
    weights.end()

    def g1(g):
        return rows[g, 2:3, :]

    def g2(g):
        return rows[g, 3:4, :]

    def wq_of(g):
        return wq[pl.ds(g * GS, GS)].reshape(GW, QKV)

    def wo_of(g):
        return wo[pl.ds(g * GS, GS)].reshape(GW, QW)

    def cd_of(g):
        return cd[pl.ds(pl.multiple_of(g * GW, GW), GW), :]

    def project_b(g, total):
        normed = (sv[g].astype(F32) * r1b * g1(g)).astype(B16)
        return total + dot(normed, wq_of(g), NN)

    qkv_b = lax.fori_loop(0, NG, project_b, jnp.zeros((TOK, QKV), F32)).astype(B16)
    kvb[own] = qkv_b[:, QW:]
    q_b = stack_heads(qkv_b[:, :QW])
    back.begin()
    codec.step(4)
    outs.x_near(-1)
    outs.x_near(1)
    outs.x_near(2)
    back.y_near()
    codec.end()

    def decode(g, total):
        stream = dot(codes_ref[...], cd_of(g), NT)
        st[g] = stream
        return total + row_sum(stream * stream)

    r1f = rms_of(lax.fori_loop(0, NG, decode, zero))

    def project_f(g, total):
        normed = (st[g] * r1f * g1(g)).astype(B16)
        return total + dot(normed, wq_of(g), NN)

    qkv_f = lax.fori_loop(0, NG, project_f, jnp.zeros((TOK, QKV), F32)).astype(B16)
    kvf[own] = qkv_f[:, QW:]
    q_f = stack_heads(qkv_f[:, :QW])
    back.x_near(0)
    back.y_far()
    fore.begin()
    for dy in (0, -1, 1, 2):
        outs.x_far(dy)
    back.x_near(-1)
    back.x_near(1)
    back.x_near(2)
    fore.y_near()

    @pl.loop(0, NG)
    def _(g):
        gm[g] = dot(grads_ref[...], cd_of(g), NT) * ENC * g2(g)

    for dy in (0, -1, 1, 2):
        back.x_far(dy)
    outs.end()
    back.end()
    fore.x_near(0)
    fore.y_far()

    q_pos = (own * TOK + lax.broadcasted_iota(jnp.int32, (1, TOK), 1)).astype(F32)
    q_pos = jnp.concatenate([q_pos] * HQ, axis=1)

    def starts(docs, index):
        zeros = D - jnp.sum(rows[:, index : index + 1, :], axis=(0, 2), keepdims=True)[0]
        return jnp.concatenate([docs * zeros] * HQ, axis=1)

    def keys_of(kv, i):
        return kv[pl.ds(i * KS, KS), :, :HD].reshape(KEYS, HD)

    def values_of(kv, i):
        return kv[pl.ds(i * KS, KS), :, HD:].reshape(KEYS, HD)

    def tops(kv, queries, start):
        def step(i, top):
            scores = dot(keys_of(kv, i), queries, NT) * SCALE
            k_pos = (
                i * KEYS + lax.broadcasted_iota(jnp.int32, (KEYS, HQ * TOK), 0)
            ).astype(F32)
            scores = jnp.where((k_pos >= start) & (k_pos <= q_pos), scores, -1e30)
            probs[i] = scores
            return jnp.maximum(top, jnp.max(scores, axis=0, keepdims=True))

        return lax.fori_loop(0, NK, step, jnp.full((1, HQ * TOK), -1e30, F32))

    def attended(kv, top):
        def step(i, carry):
            total, accum = carry
            p = jnp.exp(probs[i] - top)
            probs[i] = p
            total = total + jnp.sum(p, axis=0, keepdims=True)
            return total, accum + dot(values_of(kv, i), p.astype(B16), TN)

        total, accum = lax.fori_loop(
            0, NK, step, (jnp.zeros((1, HQ * TOK), F32), jnp.zeros((HD, HQ * TOK), F32))
        )
        return total, (accum / total).astype(B16)

    top = tops(kvb, q_b, starts(docs_b, 1))
    fore.x_near(-1)
    fore.x_near(1)
    fore.x_near(2)
    denom, att_cols = attended(kvb, top)
    att_cols = att_cols.astype(F32)
    att = from_columns(att_cols).astype(B16)

    def mix_b(g, carry):
        squares, cross = carry
        mixed = sv[g].astype(F32) + dot(att, wo_of(g), NT)
        mx[g] = mixed
        return squares + row_sum(mixed * mixed), cross + row_sum(mixed * gm[g])

    squares, cross = lax.fori_loop(0, NG, mix_b, (zero, zero))
    for dy in (0, -1, 1, 2):
        fore.x_far(dy)
    r2b = rms_of(squares)
    lean = r2b * r2b * cross * (1.0 / D)

    def grad_mix(g, total):
        grad = r2b * (gm[g] - mx[g] * lean)
        gm[g] = grad
        return total + dot(grad.astype(B16), wo_of(g), NN)

    grad_att = lax.fori_loop(0, NG, grad_mix, jnp.zeros((TOK, QW), F32)).astype(B16)
    g_heads = stack_heads(grad_att)
    delta = jnp.sum(to_columns(grad_att.astype(F32)) * att_cols, axis=0, keepdims=True)
    inverse = 1.0 / denom

    def backward_step(i, total):
        p = probs[i] * inverse
        grad_p = dot(values_of(kvb, i), g_heads, NT)
        grad_s = (p * (grad_p - delta) * SCALE).astype(B16)
        chips = pl.ds(i * (KS // NC), KS // NC)
        shape = (KS // NC, NC, TOK, HD)
        terms[chips, :, :, :HD] = dot(grad_s, q_b, NN).astype(B16).reshape(shape)
        terms[chips, :, :, HD:] = dot(p.astype(B16), g_heads, NN).astype(B16).reshape(shape)
        return total + dot(keys_of(kvb, i), grad_s, TN)

    grad_q = jnp.zeros((HD, HQ * TOK), F32)
    per = NK // NG
    for g in range(NG):
        grad_q = lax.fori_loop(g * per, (g + 1) * per, backward_step, grad_q)
        scatter.send_pair(g)
    grad_q = from_columns(grad_q).astype(B16)
    fore.end()
    scatter.along_x()

    top = tops(kvf, q_f, starts(docs_f, 0))
    scatter.x_far()
    _, att_cols = attended(kvf, top)
    att = from_columns(att_cols.astype(F32)).astype(B16)
    scatter.along_y()

    def mix_f(g, total):
        mixed = st[g] + dot(att, wo_of(g), NT)
        st[g] = mixed
        return total + row_sum(mixed * mixed)

    r2f = rms_of(lax.fori_loop(0, NG, mix_f, zero))
    scatter.y_far()

    def encode(g, total):
        normed = (st[g] * r2f * g2(g)).astype(B16)
        return total + dot(normed, cd_of(g), NN)

    coded = lax.fori_loop(0, NG, encode, jnp.zeros((TOK, R), F32))
    sent[...] = (coded * ENC).astype(B16)
    k_codes = wire.send(sent, codes_out, after)

    kv_grad = scatter.result().astype(B16)
    grad_qkv = jnp.concatenate([grad_q, kv_grad], axis=1)

    def grad_norm(g, total):
        weighted = dot(grad_qkv, wq_of(g), NT) * g1(g)
        mx[g] = weighted
        return total + row_sum(weighted * sv[g].astype(F32))

    cross = lax.fori_loop(0, NG, grad_norm, zero)
    lean1 = r1b * r1b * cross * (1.0 / D)

    def grad_code(g, total):
        grad = gm[g] + r1b * (mx[g] - sv[g].astype(F32) * lean1)
        return total + dot(grad.astype(B16), cd_of(g), NN)

    gin[...] = lax.fori_loop(0, NG, grad_code, jnp.zeros((TOK, R), F32)).astype(B16)
    k_grads = wire.send(gin, grads_out, before)
    wire.arrived(k_codes, codes_out)
    wire.arrived(k_grads, grads_out)
    wire.finish()


ANY = pl.BlockSpec(memory_space=pl.ANY)
VMEM = pl.BlockSpec(memory_space=pltpu.VMEM)


def on_device(
    codes_fwd, saved_stream, grad_codes, docs_fwd, docs_bwd, codec, wqkv, wout, gain_attn, gain_code
):
    copies = 288
    half = NYH // 2
    codes, grads = pl.pallas_call(
        tick_kernel,
        out_shape=(jax.ShapeDtypeStruct((TOK, R), B16),) * 2,
        in_specs=[VMEM, ANY, VMEM, VMEM, VMEM, VMEM, ANY, ANY, VMEM, VMEM],
        out_specs=(VMEM, VMEM),
        scratch_shapes=[
            pltpu.VMEM((NSEQ, TOK, QKV), B16),
            pltpu.VMEM((NSEQ, TOK, QW), B16),
            pltpu.VMEM((D, R), B16),
            pltpu.VMEM((NC, NX * NYH, 8, TOK), F32),
            pltpu.VMEM((NG, 8, GW), F32),
            pltpu.VMEM((NG, TOK, GW), B16),
            pltpu.VMEM((NG, TOK, GW), F32),
            pltpu.VMEM((NG, TOK, GW), F32),
            pltpu.VMEM((NG, TOK, GW), F32),
            pltpu.VMEM((NSEQ, TOK, 2 * HD), B16),
            pltpu.VMEM((NSEQ, TOK, 2 * HD), B16),
            pltpu.VMEM((NK, KEYS, HQ * TOK), F32),
            pltpu.VMEM((NX * NYH, NC, TOK, 2 * HD), B16),
            pltpu.VMEM((TOK, R), B16),
            pltpu.VMEM((TOK, R), B16),
            pltpu.VMEM((CROWS, R), B16),
            pltpu.VMEM((CROWS, R), B16),
            pltpu.VMEM((CROWS, R), B16),
            pltpu.VMEM((NX * NYH, TOK, 2 * HD), B16),
            pltpu.VMEM((NX * NYH, TOK, 2 * HD), B16),
            pltpu.VMEM((half, TOK, 2 * HD), B16),
            pltpu.VMEM((half, TOK, 2 * HD), B16),
            pltpu.VMEM((NYH, TOK, 2 * HD), B16),
            pltpu.VMEM((NYH, TOK, 2 * HD), B16),
            pltpu.VMEM((NYH, TOK, 2 * HD), B16),
            pltpu.VMEM((TOK // 2, 2 * HD), B16),
            pltpu.VMEM((TOK // 2, 2 * HD), B16),
            pltpu.VMEM((TOK, 2 * HD), B16),
            pltpu.VMEM((TOK, 2 * HD), B16),
            pltpu.SemaphoreType.DMA((copies,)),
            pltpu.SemaphoreType.DMA((copies,)),
            pltpu.SemaphoreType.DMA((3 + NG,)),
        ],
        compiler_params=pltpu.CompilerParams(
            collective_id=0, has_side_effects=True, vmem_limit_bytes=56 * 2**20
        ),
        name="tick",
    )(
        codes_fwd[0], saved_stream[0], grad_codes[0], docs_fwd, docs_bwd, codec, wqkv, wout,
        gain_attn, gain_code,
    )
    return codes[None], grads[None]


def solution(mesh):
    return jax.shard_map(
        on_device,
        mesh=mesh,
        in_specs=(
            P("section", "seq", None),
            P("section", "seq", None),
            P("section", "seq", None),
            P("section", "seq"),
            P("section", "seq"),
            P(("section", "seq"), None),
            P("section", "seq", None),
            P("section", "seq", None),
            P("section", "seq"),
            P("section", "seq"),
        ),
        out_specs=(P("section", "seq", None), P("section", "seq", None)),
        check_vma=False,
    )
```

```python
import functools

import jax
import jax.numpy as jnp
from jax import lax
from jax.experimental import pallas as pl
from jax.experimental.pallas import tpu as pltpu
from jax.sharding import PartitionSpec as P

D = 4096
R = 512
HD = 128
HQ = 2
TOK = 128
QKV = (HQ + 2) * HD
QW = HQ * HD
NX, NYH, NC = 4, 4, 2
NYL, NZ = 2, 8
NSEQ = NX * NYH * NC
NG = NX
GW = D // NG
GS = NSEQ // NG
KEYS = 512
KS = KEYS // TOK
NK = D // KEYS
SEMAPHORES = 4 * 17 + 21 + 5 + 19 + 4

EPS = 1e-05


class Place:
    def __init__(self):
        self.section = lax.axis_index("section")
        self.seq = lax.axis_index("seq")
        self.ylo = self.section // NZ
        self.z = lax.rem(self.section, NZ)
        self.x = self.seq // (NYH * NC)
        self.yh = lax.rem(self.seq // NC, NYH)
        self.c = lax.rem(self.seq, NC)

    def slot(self, dx=0, dy=0, dc=0):
        x = lax.rem(self.x + (dx + NX), NX)
        yh = lax.rem(self.yh + (dy + NYH), NYH)
        c = lax.rem(self.c + dc, NC)
        return (x * NYH + yh) * NC + c

    def chip(self, dx=0, dy=0):
        return lax.rem(self.x + (dx + NX), NX) * NYH + lax.rem(self.yh + (dy + NYH), NYH)

    def device(self, dx=0, dy=0, dc=0, dz=0, dyl=0):
        z = lax.rem(self.z + (dz + NZ), NZ)
        ylo = lax.rem(self.ylo + dyl, NYL)
        return {"section": ylo * NZ + z, "seq": self.slot(dx, dy, dc)}


class Wire:
    def __init__(self, sems):
        self.sems, self.used = sems, 0

    def new(self):
        self.used += 1
        assert self.used <= SEMAPHORES
        return self.used - 1

    def send(self, src, dst, device, out, into):
        pltpu.make_async_remote_copy(
            src_ref=src,
            dst_ref=dst,
            send_sem=self.sems.at[out],
            recv_sem=self.sems.at[into],
            device_id=device,
            device_id_type=pl.DeviceIdType.MESH,
        ).start()

    def take(self, k, ref):
        pltpu.make_async_copy(ref, ref, self.sems.at[k]).wait()


def meet(devices):
    barrier = pltpu.get_barrier_semaphore()
    for device in devices:
        pl.semaphore_signal(barrier, inc=1, device_id=device, device_id_type=pl.DeviceIdType.MESH)
    pl.semaphore_wait(barrier, len(devices))


class SectionGather:
    def __init__(self, me, wire, out, rows):
        self.me, self.wire, self.out = me, wire, out
        self.half = rows // 2
        self.sent = wire.new()
        self.y_up, self.y_down, self.y_two, self.sib = [wire.new() for _ in range(4)]
        self.x_up = {dy: wire.new() for dy in (0, -1, 1, 2)}
        self.x_down = {dy: wire.new() for dy in (0, -1, 1, 2)}
        self.x_two = {dy: wire.new() for dy in (0, -1, 1, 2)}

    def block(self, dx, dy):
        return self.out.at[self.me.slot(dx, dy)]

    def part(self, dx, dy, which):
        return self.out.at[self.me.slot(dx, dy), pl.ds(which * self.half, self.half)]

    def push(self, ref, into, **to):
        self.wire.send(ref, ref, self.me.device(**to), self.sent, into)

    def to_sibling(self, dx, dy):
        self.push(self.block(dx, dy), self.sib, dc=1)

    def begin(self):
        self.begin_y()
        self.begin_x()

    def begin_y(self):
        self.push(self.block(0, 0), self.y_up, dy=1)
        self.push(self.block(0, 0), self.y_down, dy=-1)

    def begin_x(self):
        self.along_x(0)
        self.to_sibling(0, 0)

    def along_x(self, dy):
        self.push(self.block(0, dy), self.x_up[dy], dx=1)
        self.push(self.block(0, dy), self.x_down[dy], dx=-1)

    def y_near(self):
        self.wire.take(self.y_up, self.block(0, -1))
        self.push(self.part(0, -1, 0), self.y_two, dy=1)
        self.along_x(-1)
        self.wire.take(self.y_down, self.block(0, 1))
        self.push(self.part(0, 1, 1), self.y_two, dy=-1)
        self.along_x(1)
        self.to_sibling(0, -1)
        self.to_sibling(0, 1)

    def y_far(self):
        self.wire.take(self.y_two, self.block(0, 2))
        self.along_x(2)
        self.to_sibling(0, 2)

    def x_near(self, dy):
        self.wire.take(self.x_up[dy], self.block(-1, dy))
        self.push(self.part(-1, dy, 0), self.x_two[dy], dx=1)
        self.wire.take(self.x_down[dy], self.block(1, dy))
        self.push(self.part(1, dy, 1), self.x_two[dy], dx=-1)
        self.to_sibling(-1, dy)
        self.to_sibling(1, dy)

    def x_far(self, *rows):
        for dy in rows:
            self.wire.take(self.x_two[dy], self.block(2, dy))
            self.to_sibling(2, dy)

    def end(self):
        self.wire.take(self.sib, self.out.at[pl.ds(0, NX * NYH)])

    def finish(self):
        self.wire.take(self.sent, self.out.at[pl.ds(0, NSEQ - 1)])

    def partners(self):
        me = self.me
        return [
            me.device(dy=1),
            me.device(dy=-1),
            me.device(dx=1),
            me.device(dx=-1),
            me.device(dc=1),
        ]


CROWS = 16
PLANE = NX * NYH * CROWS
LANES = R // NC


class CodecGather:
    def __init__(self, me, wire, out, both, other, tile):
        self.me, self.wire, self.out = me, wire, out
        self.both, self.other, self.tile = both, other, tile
        new = wire.new
        self.pair_out, self.pair_in, self.sent, self.sib_out, self.sib = [new() for _ in range(5)]
        self.in_y, self.in_x = new(), new()
        self.up, self.down = {}, {}
        for step in range(1, NZ // 2 + 1):
            for dyl in range(NYL):
                if step < NZ // 2 or dyl == 0:
                    self.up[dyl, step] = new()
                if step < NZ // 2 or dyl == 1:
                    self.down[dyl, step] = new()

    def ref(self, first, rows, dc=0):
        c = lax.rem(self.me.c + dc, NC)
        return self.out.at[
            pl.ds(pl.multiple_of(first, CROWS), rows),
            pl.ds(pl.multiple_of(c * LANES, LANES), LANES),
        ]

    def plane_first(self, dyl, dz):
        me = self.me
        ylo = lax.rem(me.ylo + dyl, NYL)
        return (ylo * NZ + lax.rem(me.z + (dz + NZ), NZ)) * PLANE

    def tile_ref(self, dyl, dy):
        return self.ref(self.plane_first(dyl, 0) + self.me.chip(0, dy) * CROWS, CROWS)

    def column_ref(self, dyl, dx):
        x = lax.rem(self.me.x + (dx + NX), NX)
        return self.ref(self.plane_first(dyl, 0) + x * (NYH * CROWS), NYH * CROWS)

    def plane_ref(self, dyl, dz, dc=0):
        return self.ref(self.plane_first(dyl, dz), PLANE, dc)

    def begin(self):
        me = self.me
        self.wire.send(self.both, self.other, me.device(dc=1), self.pair_out, self.pair_in)

    def pair(self, local_sem):
        me = self.me
        self.wire.take(self.pair_in, self.other)
        row = lax.broadcasted_iota(jnp.int32, (CROWS, R), 0)
        mine = (row // (CROWS // NC)) == me.c
        self.tile[...] = jnp.where(
            mine, self.both[...].astype(jnp.float32), self.other[...].astype(jnp.float32)
        ).astype(jnp.bfloat16)
        src = self.tile.at[:, pl.ds(pl.multiple_of(me.c * LANES, LANES), LANES)]
        self.local = pltpu.make_async_copy(src, self.tile_ref(0, 0), local_sem)
        self.local.start()
        for dyl in range(NYL):
            for dy in range(NYH):
                if dyl or dy:
                    to = me.device(dy=dy, dyl=dyl)
                    self.wire.send(src, self.tile_ref(0, 0), to, self.sent, self.in_y)

    def columns(self):
        me = self.me
        self.local.wait()
        self.wire.take(self.in_y, self.out.at[pl.ds(0, (NYL * NYH - 1) * CROWS), pl.ds(0, LANES)])
        for dx in (1, -1, 2):
            for dyl in range(NYL):
                ref = self.column_ref(dyl, 0)
                self.wire.send(ref, ref, me.device(dx=dx), self.sent, self.in_x)

    def planes(self):
        rows = (NX - 1) * NYL * NYH * CROWS
        self.wire.take(self.in_x, self.out.at[pl.ds(0, rows), pl.ds(0, LANES)])
        for dyl in range(NYL):
            self.pass_on(dyl, 0)

    def pass_on(self, dyl, step):
        me = self.me
        below, above = self.plane_ref(dyl, -step), self.plane_ref(dyl, step)
        if (dyl, step + 1) in self.up:
            self.wire.send(below, below, me.device(dz=1), self.sent, self.up[dyl, step + 1])
        if (dyl, step + 1) in self.down:
            self.wire.send(above, above, me.device(dz=-1), self.sent, self.down[dyl, step + 1])
        self.to_sibling(dyl, -step)
        if step:
            self.to_sibling(dyl, step)

    def to_sibling(self, dyl, dz):
        ref = self.plane_ref(dyl, dz)
        self.wire.send(ref, ref, self.me.device(dc=1), self.sib_out, self.sib)

    def step(self, step):
        for dyl in range(NYL):
            if step < NZ // 2:
                self.wire.take(self.up[dyl, step], self.plane_ref(dyl, -step))
                self.wire.take(self.down[dyl, step], self.plane_ref(dyl, step))
                self.pass_on(dyl, step)
            else:
                keys = self.up if dyl == 0 else self.down
                self.wire.take(keys[dyl, step], self.plane_ref(dyl, step))
                self.to_sibling(dyl, step)

    def end(self):
        self.wire.take(self.sib, self.out.at[:, pl.ds(0, LANES)])

    def finish(self):
        rows = 7 * CROWS + 6 * NYH * CROWS + 14 * PLANE
        self.wire.take(self.pair_out, self.both)
        self.wire.take(self.sent, self.out.at[pl.ds(0, rows), pl.ds(0, LANES)])
        self.wire.take(self.sib_out, self.out.at[:, pl.ds(0, LANES)])

    def partners(self):
        me = self.me
        return [
            me.device(dy=2),
            me.device(dx=2),
            me.device(dz=1),
            me.device(dz=-1),
        ] + [me.device(dyl=1, dy=dy) for dy in range(NYH)]


class MetaGather:
    def __init__(self, me, wire, buf):
        self.me, self.wire, self.buf = me, wire, buf
        self.sent, self.in_y, self.in_x, self.sib_out, self.sib = [wire.new() for _ in range(5)]

    def column(self, dx):
        x = lax.rem(self.me.x + (dx + NX), NX)
        return self.buf.at[self.me.c, pl.ds(x * NYH, NYH)]

    def begin(self):
        me = self.me
        ref = self.buf.at[me.c, me.chip()]
        for dy in (1, -1, 2):
            self.wire.send(ref, ref, me.device(dy=dy), self.sent, self.in_y)

    def columns(self):
        me = self.me
        self.wire.take(self.in_y, self.buf.at[0, pl.ds(0, NYH - 1)])
        ref = self.column(0)
        for dx in (1, -1, 2):
            self.wire.send(ref, ref, me.device(dx=dx), self.sent, self.in_x)

    def pair(self):
        me = self.me
        self.wire.take(self.in_x, self.buf.at[0, pl.ds(0, (NX - 1) * NYH)])
        ref = self.buf.at[me.c]
        self.wire.send(ref, ref, me.device(dc=1), self.sib_out, self.sib)

    def end(self):
        self.wire.take(self.sib, self.buf.at[0])

    def finish(self):
        self.wire.take(self.sent, self.buf.at[0, pl.ds(0, NYH - 1 + (NX - 1) * NYH)])
        self.wire.take(self.sib_out, self.buf.at[0])


def add_into(dst, *others):
    total = dst[...].astype(jnp.float32)
    for other in others:
        total = total + other[...].astype(jnp.float32)
    dst[...] = total.astype(dst.dtype)


class TermScatter:
    def __init__(self, me, wire, terms, bufs):
        self.me, self.wire, self.terms = me, wire, terms
        (self.pair, self.part, self.far_up, self.far_down, self.near_up, self.near_down,
         self.row, self.yfar_up, self.yfar_down, self.ynear_up, self.ynear_down) = bufs
        new = wire.new
        self.pair_out, self.x_out, self.y_out = new(), new(), new()
        self.pair_in = {dx: new() for dx in (2, 1, -1, 0)}
        self.x_in, self.y_in = [new() for _ in range(6)], [new() for _ in range(6)]

    def at_x(self, dx):
        return lax.rem(self.me.x + (dx + NX), NX) * NYH

    def group(self, dx, first=0, count=NYH):
        return self.part.at[pl.ds(self.at_x(dx) + first, count)]

    def send_pair(self, dx):
        chips = pl.ds(self.at_x(dx), NYH)
        self.wire.send(
            self.terms.at[chips, 1 - self.me.c], self.pair.at[chips],
            self.me.device(dc=1), self.pair_out, self.pair_in[dx],
        )

    def add_pair(self, dx):
        first = self.at_x(dx)
        self.wire.take(self.pair_in[dx], self.pair.at[pl.ds(first, NYH)])
        for j in range(NYH):
            i = first + j
            self.part[i] = (
                self.terms[i, self.me.c].astype(jnp.float32) + self.pair[i].astype(jnp.float32)
            ).astype(jnp.bfloat16)

    def send_x(self, src, dst, k, dx):
        self.wire.send(src, dst, self.me.device(dx=dx), self.x_out, self.x_in[k])

    def x_start(self):
        half = NYH // 2
        self.send_x(self.group(2, 0, half), self.far_up, 0, 1)
        self.send_x(self.group(2, half, half), self.far_down, 1, -1)

    def x_up(self):
        half = NYH // 2
        self.send_x(self.group(1, half, half), self.near_up.at[pl.ds(half, half)], 2, 1)

    def x_down(self):
        half = NYH // 2
        self.send_x(self.group(-1, 0, half), self.near_down.at[pl.ds(0, half)], 3, -1)

    def x_far(self):
        half = NYH // 2
        self.wire.take(self.x_in[0], self.far_up)
        add_into(self.group(1, 0, half), self.far_up)
        self.send_x(self.group(1, 0, half), self.near_up.at[pl.ds(0, half)], 4, 1)
        self.wire.take(self.x_in[1], self.far_down)
        add_into(self.group(-1, half, half), self.far_down)
        self.send_x(self.group(-1, half, half), self.near_down.at[pl.ds(half, half)], 5, -1)

    def at_y(self, dy):
        return lax.rem(self.me.yh + (dy + NYH), NYH)

    def send_y(self, src, dst, k, dy):
        self.wire.send(src, dst, self.me.device(dy=dy), self.y_out, self.y_in[k])

    def along_y(self):
        half = NYH // 2
        for k, ref in ((2, self.near_up), (3, self.near_down), (4, self.near_up), (5, self.near_down)):
            self.wire.take(self.x_in[k], ref.at[pl.ds(0, half)])
        mine = self.at_x(0)
        row = self.row
        for i in range(NYH):
            row[i] = (
                self.part[mine + i].astype(jnp.float32)
                + self.near_up[i].astype(jnp.float32)
                + self.near_down[i].astype(jnp.float32)
            ).astype(jnp.bfloat16)
        rows = TOK // 2
        low, high = pl.ds(0, rows), pl.ds(rows, rows)
        at_y = self.at_y
        self.send_y(row.at[at_y(2), low], self.yfar_up, 0, 1)
        self.send_y(row.at[at_y(2), high], self.yfar_down, 1, -1)
        self.send_y(row.at[at_y(1), high], self.ynear_up.at[high], 2, 1)
        self.send_y(row.at[at_y(-1), low], self.ynear_down.at[low], 3, -1)

    def y_far(self):
        row, at_y = self.row, self.at_y
        rows = TOK // 2
        low, high = pl.ds(0, rows), pl.ds(rows, rows)
        self.wire.take(self.y_in[0], self.yfar_up)
        add_into(row.at[at_y(1), low], self.yfar_up)
        self.send_y(row.at[at_y(1), low], self.ynear_up.at[low], 4, 1)
        self.wire.take(self.y_in[1], self.yfar_down)
        add_into(row.at[at_y(-1), high], self.yfar_down)
        self.send_y(row.at[at_y(-1), high], self.ynear_down.at[high], 5, -1)

    def result(self):
        rows = TOK // 2
        low, high = pl.ds(0, rows), pl.ds(rows, rows)
        self.wire.take(self.y_in[2], self.ynear_up.at[high])
        self.wire.take(self.y_in[3], self.ynear_down.at[low])
        self.wire.take(self.y_in[4], self.ynear_up.at[low])
        self.wire.take(self.y_in[5], self.ynear_down.at[high])
        return (
            self.row[self.at_y(0)].astype(jnp.float32)
            + self.ynear_up[...].astype(jnp.float32)
            + self.ynear_down[...].astype(jnp.float32)
        )

    def finish(self):
        self.wire.take(self.pair_out, self.pair)
        self.wire.take(self.x_out, self.part.at[pl.ds(0, NX * NYH - NYH)])
        self.wire.take(self.y_out, self.row.at[pl.ds(0, NYH - 1)])


def dot(a, b, dims):
    return lax.dot_general(a, b, (dims, ((), ())), preferred_element_type=jnp.float32)


NN = ((1,), (0,))
NT = ((1,), (1,))
TN = ((0,), (0,))
F32, B16 = jnp.float32, jnp.bfloat16
SCALE = HD ** (-0.5)
ENC = (R / D) ** 0.5


def row_sum(values):
    return jnp.sum(values, axis=-1, keepdims=True)


def rms_of(total):
    return lax.rsqrt(total * (1.0 / D) + EPS)


def stack_heads(matrix):
    return jnp.concatenate([matrix[:, h * HD : (h + 1) * HD] for h in range(HQ)], axis=0)


def from_columns(columns):
    return jnp.concatenate(
        [columns[:, h * TOK : (h + 1) * TOK].T for h in range(HQ)], axis=1
    )


def to_columns(matrix):
    return jnp.concatenate([matrix[:, h * HD : (h + 1) * HD].T for h in range(HQ)], axis=1)


def tick_kernel(
    codes_ref, saved_ref, grads_ref, docs_f_ref, docs_b_ref, codec_ref, wqkv_ref, wout_ref,
    g1_ref, g2_ref,
    codes_out, grads_out,
    wk, wo, cd, meta, rows, sv, nb, st, gm, mx, kvf, kvb, probs, terms, codes, grads, sent, gin,
    both, other, tile,
    pair, part, far_up, far_down, near_up, near_down, row, yfar_up, yfar_down, ynear_up, ynear_down,
    sems, local_sems,
):
    me = Place()
    wire = Wire(sems)
    first = SectionGather(me, wire, wk, TOK)
    second = SectionGather(me, wire, wo, TOK)
    codec = CodecGather(me, wire, cd, both, other, tile)
    metas = MetaGather(me, wire, meta)
    back = SectionGather(me, wire, kvb, TOK)
    fore = SectionGather(me, wire, kvf, TOK)
    scatter = TermScatter(
        me, wire, terms,
        (pair, part, far_up, far_down, near_up, near_down, row,
         yfar_up, yfar_down, ynear_up, ynear_down),
    )
    codes_sent, codes_in, grads_sent, grads_in = [wire.new() for _ in range(4)]
    own = me.slot()
    sections = NYL * NZ
    after = {"section": lax.rem(me.section + 1, sections), "seq": me.seq}
    before = {"section": lax.rem(me.section + sections - 1, sections), "seq": me.seq}
    everyone = (0, -1, 1, 2)

    fills = []

    def fill(src, dst):
        copy = pltpu.make_async_copy(src, dst, local_sems.at[len(fills)])
        copy.start()
        fills.append(copy)
        return copy

    fill_k = fill(wqkv_ref.at[0, :, pl.ds(QW, 2 * HD)], wk.at[own])
    fill_w = [
        fill(wqkv_ref.at[0, :, pl.ds(0, QW)], wo.at[own, :, pl.ds(0, QW)]),
        fill(wout_ref.at[0], wo.at[own, :, pl.ds(QW, QW)]),
    ]
    fill_x = [fill(saved_ref.at[:, pl.ds(g * GW, GW)], sv.at[g]) for g in range(NG)]
    fill_x += [fill(codes_ref, codes), fill(grads_ref, grads)]
    tall = codec_ref[...].astype(F32)
    both[...] = jnp.concatenate([tall, tall], axis=0).astype(B16)
    docs_f, docs_b = docs_f_ref[...].astype(F32), docs_b_ref[...].astype(F32)
    meta[me.c, me.chip()] = jnp.concatenate(
        [docs_f, docs_b, g1_ref[...].astype(F32), g2_ref[...].astype(F32), jnp.zeros((4, TOK), F32)],
        axis=0,
    )
    meet(first.partners() + codec.partners() + [after, before])
    fill_k.wait()
    first.begin()
    codec.begin()
    metas.begin()
    for copy in fill_w:
        copy.wait()
    second.begin_x()
    for copy in fill_x:
        copy.wait()

    def square_step(g, total):
        values = sv[g].astype(F32)
        return total + row_sum(values * values)

    zero = jnp.zeros((TOK, 1), F32)
    codec.pair(local_sems.at[len(fills)])
    r1b = rms_of(lax.fori_loop(0, NG, square_step, zero))
    metas.columns()
    first.x_near(0)
    first.y_near()
    second.begin_y()
    codec.columns()
    second.x_near(0)
    metas.pair()
    first.y_far()
    first.x_near(-1)
    first.x_near(1)
    codec.planes()
    metas.end()
    for q in range(NSEQ):
        rows[q // GS, :, q % GS * TOK : (q % GS + 1) * TOK] = meta[q % NC, q // NC]

    def g1(g):
        return rows[g, 2:3, :]

    def g2(g):
        return rows[g, 3:4, :]

    @pl.loop(0, NG)
    def _(g):
        nb[g] = (sv[g].astype(F32) * r1b * g1(g)).astype(B16)

    first.x_far(0)
    first.x_near(2)
    second.y_near()
    first.x_far(-1, 1, 2)
    first.end()

    def wk_of(g):
        return wk[pl.ds(g * GS, GS)].reshape(GW, 2 * HD)

    def wq_of(g):
        return wo[pl.ds(g * GS, GS), :, :QW].reshape(GW, QW)

    def wo_of(g):
        return wo[pl.ds(g * GS, GS), :, QW:].reshape(GW, QW)

    def cd_of(g):
        return cd[pl.ds(pl.multiple_of(g * GW, GW), GW), :]

    def project(values, weights_of):
        def step(g, total):
            return total + dot(values[g], weights_of(g), NN)

        return lax.fori_loop(0, NG, step, jnp.zeros((TOK, QW), F32)).astype(B16)

    kvb[own] = project(nb, wk_of)
    back.begin()
    second.y_far()
    second.x_near(-1)
    second.x_near(1)
    codec.step(1)
    back.x_near(0)
    back.y_near()
    second.x_near(2)
    codec.step(2)
    back.y_far()
    second.x_far(*everyone)
    back.x_near(-1)
    back.x_near(1)
    codec.step(3)
    back.x_near(2)
    second.end()
    q_b = stack_heads(project(nb, wq_of))
    back.x_far(*everyone)
    codec.step(4)
    codec.end()

    def decode(g, total):
        stream = dot(codes[...], cd_of(g), NT)
        st[g] = stream
        return total + row_sum(stream * stream)

    r1f = rms_of(lax.fori_loop(0, NG, decode, zero))

    @pl.loop(0, NG)
    def _(g):
        nb[g] = (st[g] * r1f * g1(g)).astype(B16)

    kvf[own] = project(nb, wk_of)
    fore.begin()
    q_f = stack_heads(project(nb, wq_of))
    back.end()

    q_pos = (own * TOK + lax.broadcasted_iota(jnp.int32, (1, TOK), 1)).astype(F32)
    q_pos = jnp.concatenate([q_pos] * HQ, axis=1)

    def starts(docs, index):
        zeros = D - jnp.sum(rows[:, index : index + 1, :], axis=(0, 2), keepdims=True)[0]
        return jnp.concatenate([docs * zeros] * HQ, axis=1)

    def keys_of(kv, i):
        return kv[pl.ds(i * KS, KS), :, :HD].reshape(KEYS, HD)

    def values_of(kv, i):
        return kv[pl.ds(i * KS, KS), :, HD:].reshape(KEYS, HD)

    def tops(kv, queries, start):
        def step(i, top):
            scores = dot(keys_of(kv, i), queries, NT) * SCALE
            k_pos = (
                i * KEYS + lax.broadcasted_iota(jnp.int32, (KEYS, HQ * TOK), 0)
            ).astype(F32)
            scores = jnp.where((k_pos >= start) & (k_pos <= q_pos), scores, -1e30)
            probs[i] = scores
            return jnp.maximum(top, jnp.max(scores, axis=0, keepdims=True))

        return lax.fori_loop(0, NK, step, jnp.full((1, HQ * TOK), -1e30, F32))

    def attended(kv, top):
        def step(i, carry):
            total, accum = carry
            p = jnp.exp(probs[i] - top)
            probs[i] = p
            total = total + jnp.sum(p, axis=0, keepdims=True)
            return total, accum + dot(values_of(kv, i), p.astype(B16), TN)

        total, accum = lax.fori_loop(
            0, NK, step, (jnp.zeros((1, HQ * TOK), F32), jnp.zeros((HD, HQ * TOK), F32))
        )
        return total, (accum / total).astype(B16)

    top = tops(kvb, q_b, starts(docs_b, 1))
    denom, att_cols = attended(kvb, top)
    att_cols = att_cols.astype(F32)
    att = from_columns(att_cols).astype(B16)

    @pl.loop(0, NG)
    def _(g):
        gm[g] = dot(grads[...], cd_of(g), NT) * ENC * g2(g)

    fore.x_near(0)
    fore.y_near()

    def mix_b(g, carry):
        squares, cross = carry
        mixed = sv[g].astype(F32) + dot(att, wo_of(g), NT)
        mx[g] = mixed
        return squares + row_sum(mixed * mixed), cross + row_sum(mixed * gm[g])

    squares, cross = lax.fori_loop(0, NG, mix_b, (zero, zero))
    r2b = rms_of(squares)
    lean = r2b * r2b * cross * (1.0 / D)
    fore.y_far()

    def grad_mix(g, total):
        grad = r2b * (gm[g] - mx[g] * lean)
        gm[g] = grad
        return total + dot(grad.astype(B16), wo_of(g), NN)

    grad_att = lax.fori_loop(0, NG, grad_mix, jnp.zeros((TOK, QW), F32)).astype(B16)
    g_heads = stack_heads(grad_att)
    delta = jnp.sum(to_columns(grad_att.astype(F32)) * att_cols, axis=0, keepdims=True)
    inverse = 1.0 / denom

    def backward_step(i, total):
        p = probs[i] * inverse
        grad_p = dot(values_of(kvb, i), g_heads, NT)
        grad_s = (p * (grad_p - delta) * SCALE).astype(B16)
        chips = pl.ds(i * (KS // NC), KS // NC)
        shape = (KS // NC, NC, TOK, HD)
        terms[chips, :, :, :HD] = dot(grad_s, q_b, NN).astype(B16).reshape(shape)
        terms[chips, :, :, HD:] = dot(p.astype(B16), g_heads, NN).astype(B16).reshape(shape)
        return total + dot(keys_of(kvb, i), grad_s, TN)

    grad_q = jnp.zeros((HD, HQ * TOK), F32)
    per = NK // NG

    def backward(dx, total):
        g = lax.rem(me.x + (dx + NX), NX)
        total = lax.fori_loop(g * per, (g + 1) * per, backward_step, total)
        scatter.send_pair(dx)
        return total

    grad_q = backward(2, grad_q)
    fore.x_near(-1)
    grad_q = backward(1, grad_q)
    scatter.add_pair(2)
    scatter.x_start()
    fore.x_near(1)
    grad_q = backward(-1, grad_q)
    scatter.add_pair(1)
    scatter.x_up()
    fore.x_near(2)
    grad_q = backward(0, grad_q)
    scatter.add_pair(-1)
    scatter.x_down()
    scatter.x_far()
    fore.x_far(*everyone)
    scatter.add_pair(0)
    grad_q = from_columns(grad_q).astype(B16)
    fore.end()

    top = tops(kvf, q_f, starts(docs_f, 0))
    scatter.along_y()
    _, att_cols = attended(kvf, top)
    att = from_columns(att_cols.astype(F32)).astype(B16)
    scatter.y_far()

    def mix_f(g, total):
        mixed = st[g] + dot(att, wo_of(g), NT)
        st[g] = mixed
        return total + row_sum(mixed * mixed)

    r2f = rms_of(lax.fori_loop(0, NG, mix_f, zero))

    def encode(g, total):
        normed = (st[g] * r2f * g2(g)).astype(B16)
        return total + dot(normed, cd_of(g), NN)

    coded = lax.fori_loop(0, NG, encode, jnp.zeros((TOK, R), F32))
    sent[...] = (coded * ENC).astype(B16)
    wire.send(sent, codes_out, after, codes_sent, codes_in)

    kv_grad = scatter.result().astype(B16)

    def grad_norm(g, total):
        weighted = (dot(grad_q, wq_of(g), NT) + dot(kv_grad, wk_of(g), NT)) * g1(g)
        mx[g] = weighted
        return total + row_sum(weighted * sv[g].astype(F32))

    cross = lax.fori_loop(0, NG, grad_norm, zero)
    lean1 = r1b * r1b * cross * (1.0 / D)

    def grad_code(g, total):
        grad = gm[g] + r1b * (mx[g] - sv[g].astype(F32) * lean1)
        return total + dot(grad.astype(B16), cd_of(g), NN)

    gin[...] = lax.fori_loop(0, NG, grad_code, jnp.zeros((TOK, R), F32)).astype(B16)
    wire.send(gin, grads_out, before, grads_sent, grads_in)
    for gather in (first, second, codec, metas, back, fore, scatter):
        gather.finish()
    wire.take(codes_sent, sent)
    wire.take(codes_in, codes_out)
    wire.take(grads_sent, gin)
    wire.take(grads_in, grads_out)


ANY = pl.BlockSpec(memory_space=pl.ANY)
VMEM = pl.BlockSpec(memory_space=pltpu.VMEM)


def on_device(
    codes_fwd, saved_stream, grad_codes, docs_fwd, docs_bwd, codec, wqkv, wout, gain_attn, gain_code
):
    half = NYH // 2
    codes, grads = pl.pallas_call(
        tick_kernel,
        out_shape=(jax.ShapeDtypeStruct((TOK, R), B16),) * 2,
        in_specs=[ANY, ANY, ANY, VMEM, VMEM, VMEM, ANY, ANY, VMEM, VMEM],
        out_specs=(VMEM, VMEM),
        scratch_shapes=[
            pltpu.VMEM((NSEQ, TOK, 2 * HD), B16),
            pltpu.VMEM((NSEQ, TOK, 2 * QW), B16),
            pltpu.VMEM((D, R), B16),
            pltpu.VMEM((NC, NX * NYH, 8, TOK), F32),
            pltpu.VMEM((NG, 8, GW), F32),
            pltpu.VMEM((NG, TOK, GW), B16),
            pltpu.VMEM((NG, TOK, GW), B16),
            pltpu.VMEM((NG, TOK, GW), F32),
            pltpu.VMEM((NG, TOK, GW), F32),
            pltpu.VMEM((NG, TOK, GW), F32),
            pltpu.VMEM((NSEQ, TOK, 2 * HD), B16),
            pltpu.VMEM((NSEQ, TOK, 2 * HD), B16),
            pltpu.VMEM((NK, KEYS, HQ * TOK), F32),
            pltpu.VMEM((NX * NYH, NC, TOK, 2 * HD), B16),
            pltpu.VMEM((TOK, R), B16),
            pltpu.VMEM((TOK, R), B16),
            pltpu.VMEM((TOK, R), B16),
            pltpu.VMEM((TOK, R), B16),
            pltpu.VMEM((CROWS, R), B16),
            pltpu.VMEM((CROWS, R), B16),
            pltpu.VMEM((CROWS, R), B16),
            pltpu.VMEM((NX * NYH, TOK, 2 * HD), B16),
            pltpu.VMEM((NX * NYH, TOK, 2 * HD), B16),
            pltpu.VMEM((half, TOK, 2 * HD), B16),
            pltpu.VMEM((half, TOK, 2 * HD), B16),
            pltpu.VMEM((NYH, TOK, 2 * HD), B16),
            pltpu.VMEM((NYH, TOK, 2 * HD), B16),
            pltpu.VMEM((NYH, TOK, 2 * HD), B16),
            pltpu.VMEM((TOK // 2, 2 * HD), B16),
            pltpu.VMEM((TOK // 2, 2 * HD), B16),
            pltpu.VMEM((TOK, 2 * HD), B16),
            pltpu.VMEM((TOK, 2 * HD), B16),
            pltpu.SemaphoreType.DMA((SEMAPHORES,)),
            pltpu.SemaphoreType.DMA((10,)),
        ],
        compiler_params=pltpu.CompilerParams(
            collective_id=0, has_side_effects=True, vmem_limit_bytes=56 * 2**20
        ),
        name="tick",
    )(
        codes_fwd[0], saved_stream[0], grad_codes[0], docs_fwd, docs_bwd, codec, wqkv, wout,
        gain_attn, gain_code,
    )
    return codes[None], grads[None]


def solution(mesh):
    return jax.shard_map(
        on_device,
        mesh=mesh,
        in_specs=(
            P("section", "seq", None),
            P("section", "seq", None),
            P("section", "seq", None),
            P("section", "seq"),
            P("section", "seq"),
            P(("section", "seq"), None),
            P("section", "seq", None),
            P("section", "seq", None),
            P("section", "seq"),
            P("section", "seq"),
        ),
        out_specs=(P("section", "seq", None), P("section", "seq", None)),
        check_vma=False,
    )
```

```python
import functools

import jax
import jax.numpy as jnp
from jax import lax
from jax.experimental import pallas as pl
from jax.experimental.pallas import tpu as pltpu
from jax.sharding import PartitionSpec as P

D = 4096
R = 512
HD = 128
HQ = 2
TOK = 128
QKV = (HQ + 2) * HD
QW = HQ * HD
NX, NYH, NC = 4, 4, 2
NYL, NZ = 2, 8
NSEQ = NX * NYH * NC
NG = NX
GW = D // NG
GS = NSEQ // NG
KEYS = 512
KS = KEYS // TOK
NK = D // KEYS
SEMAPHORES = 4 * 17 + 21 + 5 + 19 + 4

EPS = 1e-05


class Place:
    def __init__(self):
        self.section = lax.axis_index("section")
        self.seq = lax.axis_index("seq")
        self.ylo = self.section // NZ
        self.z = lax.rem(self.section, NZ)
        self.x = self.seq // (NYH * NC)
        self.yh = lax.rem(self.seq // NC, NYH)
        self.c = lax.rem(self.seq, NC)

    def slot(self, dx=0, dy=0, dc=0):
        x = lax.rem(self.x + (dx + NX), NX)
        yh = lax.rem(self.yh + (dy + NYH), NYH)
        c = lax.rem(self.c + dc, NC)
        return (x * NYH + yh) * NC + c

    def chip(self, dx=0, dy=0):
        return lax.rem(self.x + (dx + NX), NX) * NYH + lax.rem(self.yh + (dy + NYH), NYH)

    def device(self, dx=0, dy=0, dc=0, dz=0, dyl=0):
        z = lax.rem(self.z + (dz + NZ), NZ)
        ylo = lax.rem(self.ylo + dyl, NYL)
        return {"section": ylo * NZ + z, "seq": self.slot(dx, dy, dc)}


class Wire:
    def __init__(self, sems):
        self.sems, self.used = sems, 0

    def new(self):
        self.used += 1
        assert self.used <= SEMAPHORES
        return self.used - 1

    def send(self, src, dst, device, out, into):
        pltpu.make_async_remote_copy(
            src_ref=src,
            dst_ref=dst,
            send_sem=self.sems.at[out],
            recv_sem=self.sems.at[into],
            device_id=device,
            device_id_type=pl.DeviceIdType.MESH,
        ).start()

    def take(self, k, ref):
        pltpu.make_async_copy(ref, ref, self.sems.at[k]).wait()


def meet(devices):
    barrier = pltpu.get_barrier_semaphore()
    for device in devices:
        pl.semaphore_signal(barrier, inc=1, device_id=device, device_id_type=pl.DeviceIdType.MESH)
    pl.semaphore_wait(barrier, len(devices))


class SectionGather:
    def __init__(self, me, wire, out, rows):
        self.me, self.wire, self.out = me, wire, out
        self.half = rows // 2
        self.sent = wire.new()
        self.y_up, self.y_down, self.y_two, self.sib = [wire.new() for _ in range(4)]
        self.x_up = {dy: wire.new() for dy in (0, -1, 1, 2)}
        self.x_down = {dy: wire.new() for dy in (0, -1, 1, 2)}
        self.x_two = {dy: wire.new() for dy in (0, -1, 1, 2)}

    def block(self, dx, dy):
        return self.out.at[self.me.slot(dx, dy)]

    def part(self, dx, dy, which):
        return self.out.at[self.me.slot(dx, dy), pl.ds(which * self.half, self.half)]

    def push(self, ref, into, **to):
        self.wire.send(ref, ref, self.me.device(**to), self.sent, into)

    def to_sibling(self, dx, dy):
        self.push(self.block(dx, dy), self.sib, dc=1)

    def begin(self):
        self.begin_y()
        self.begin_x()

    def begin_y(self):
        self.push(self.block(0, 0), self.y_up, dy=1)
        self.push(self.block(0, 0), self.y_down, dy=-1)

    def begin_x(self):
        self.along_x(0)
        self.to_sibling(0, 0)

    def along_x(self, dy):
        self.push(self.block(0, dy), self.x_up[dy], dx=1)
        self.push(self.block(0, dy), self.x_down[dy], dx=-1)

    def y_near(self):
        self.wire.take(self.y_up, self.block(0, -1))
        self.push(self.part(0, -1, 0), self.y_two, dy=1)
        self.along_x(-1)
        self.wire.take(self.y_down, self.block(0, 1))
        self.push(self.part(0, 1, 1), self.y_two, dy=-1)
        self.along_x(1)
        self.to_sibling(0, -1)
        self.to_sibling(0, 1)

    def y_far(self):
        self.wire.take(self.y_two, self.block(0, 2))
        self.along_x(2)
        self.to_sibling(0, 2)

    def x_near(self, dy):
        self.wire.take(self.x_up[dy], self.block(-1, dy))
        self.push(self.part(-1, dy, 0), self.x_two[dy], dx=1)
        self.wire.take(self.x_down[dy], self.block(1, dy))
        self.push(self.part(1, dy, 1), self.x_two[dy], dx=-1)
        self.to_sibling(-1, dy)
        self.to_sibling(1, dy)

    def x_far(self, *rows):
        for dy in rows:
            self.wire.take(self.x_two[dy], self.block(2, dy))
            self.to_sibling(2, dy)

    def end(self):
        self.wire.take(self.sib, self.out.at[pl.ds(0, NX * NYH)])

    def finish(self):
        self.wire.take(self.sent, self.out.at[pl.ds(0, NSEQ - 1)])

    def partners(self):
        me = self.me
        return [
            me.device(dy=1),
            me.device(dy=-1),
            me.device(dx=1),
            me.device(dx=-1),
            me.device(dc=1),
        ]


CROWS = 16
PLANE = NX * NYH * CROWS
LANES = R // NC


class CodecGather:
    def __init__(self, me, wire, out, both, other, tile):
        self.me, self.wire, self.out = me, wire, out
        self.both, self.other, self.tile = both, other, tile
        new = wire.new
        self.pair_out, self.pair_in, self.sent, self.sib_out, self.sib = [new() for _ in range(5)]
        self.in_y, self.in_x = new(), new()
        self.up, self.down = {}, {}
        for step in range(1, NZ // 2 + 1):
            for dyl in range(NYL):
                if step < NZ // 2 or dyl == 0:
                    self.up[dyl, step] = new()
                if step < NZ // 2 or dyl == 1:
                    self.down[dyl, step] = new()

    def ref(self, first, rows, dc=0):
        c = lax.rem(self.me.c + dc, NC)
        return self.out.at[
            pl.ds(pl.multiple_of(first, CROWS), rows),
            pl.ds(pl.multiple_of(c * LANES, LANES), LANES),
        ]

    def plane_first(self, dyl, dz):
        me = self.me
        ylo = lax.rem(me.ylo + dyl, NYL)
        return (ylo * NZ + lax.rem(me.z + (dz + NZ), NZ)) * PLANE

    def tile_ref(self, dyl, dy):
        return self.ref(self.plane_first(dyl, 0) + self.me.chip(0, dy) * CROWS, CROWS)

    def column_ref(self, dyl, dx):
        x = lax.rem(self.me.x + (dx + NX), NX)
        return self.ref(self.plane_first(dyl, 0) + x * (NYH * CROWS), NYH * CROWS)

    def plane_ref(self, dyl, dz, dc=0):
        return self.ref(self.plane_first(dyl, dz), PLANE, dc)

    def begin(self):
        me = self.me
        self.wire.send(self.both, self.other, me.device(dc=1), self.pair_out, self.pair_in)

    def pair(self, local_sem):
        me = self.me
        self.wire.take(self.pair_in, self.other)
        row = lax.broadcasted_iota(jnp.int32, (CROWS, R), 0)
        mine = (row // (CROWS // NC)) == me.c
        self.tile[...] = jnp.where(
            mine, self.both[...].astype(jnp.float32), self.other[...].astype(jnp.float32)
        ).astype(jnp.bfloat16)
        src = self.tile.at[:, pl.ds(pl.multiple_of(me.c * LANES, LANES), LANES)]
        self.local = pltpu.make_async_copy(src, self.tile_ref(0, 0), local_sem)
        self.local.start()
        for dyl in range(NYL):
            for dy in range(NYH):
                if dyl or dy:
                    to = me.device(dy=dy, dyl=dyl)
                    self.wire.send(src, self.tile_ref(0, 0), to, self.sent, self.in_y)

    def columns(self):
        me = self.me
        self.local.wait()
        self.wire.take(self.in_y, self.out.at[pl.ds(0, (NYL * NYH - 1) * CROWS), pl.ds(0, LANES)])
        for dx in (1, -1, 2):
            for dyl in range(NYL):
                ref = self.column_ref(dyl, 0)
                self.wire.send(ref, ref, me.device(dx=dx), self.sent, self.in_x)

    def planes(self):
        rows = (NX - 1) * NYL * NYH * CROWS
        self.wire.take(self.in_x, self.out.at[pl.ds(0, rows), pl.ds(0, LANES)])
        for dyl in range(NYL):
            self.pass_on(dyl, 0)

    def pass_on(self, dyl, step):
        me = self.me
        below, above = self.plane_ref(dyl, -step), self.plane_ref(dyl, step)
        if (dyl, step + 1) in self.up:
            self.wire.send(below, below, me.device(dz=1), self.sent, self.up[dyl, step + 1])
        if (dyl, step + 1) in self.down:
            self.wire.send(above, above, me.device(dz=-1), self.sent, self.down[dyl, step + 1])
        self.to_sibling(dyl, -step)
        if step:
            self.to_sibling(dyl, step)

    def to_sibling(self, dyl, dz):
        ref = self.plane_ref(dyl, dz)
        self.wire.send(ref, ref, self.me.device(dc=1), self.sib_out, self.sib)

    def step(self, step):
        for dyl in range(NYL):
            if step < NZ // 2:
                self.wire.take(self.up[dyl, step], self.plane_ref(dyl, -step))
                self.wire.take(self.down[dyl, step], self.plane_ref(dyl, step))
                self.pass_on(dyl, step)
            else:
                keys = self.up if dyl == 0 else self.down
                self.wire.take(keys[dyl, step], self.plane_ref(dyl, step))
                self.to_sibling(dyl, step)

    def end(self):
        self.wire.take(self.sib, self.out.at[:, pl.ds(0, LANES)])

    def finish(self):
        rows = 7 * CROWS + 6 * NYH * CROWS + 14 * PLANE
        self.wire.take(self.pair_out, self.both)
        self.wire.take(self.sent, self.out.at[pl.ds(0, rows), pl.ds(0, LANES)])
        self.wire.take(self.sib_out, self.out.at[:, pl.ds(0, LANES)])

    def partners(self):
        me = self.me
        return [
            me.device(dy=2),
            me.device(dx=2),
            me.device(dz=1),
            me.device(dz=-1),
        ] + [me.device(dyl=1, dy=dy) for dy in range(NYH)]


class MetaGather:
    def __init__(self, me, wire, buf):
        self.me, self.wire, self.buf = me, wire, buf
        self.sent, self.in_y, self.in_x, self.sib_out, self.sib = [wire.new() for _ in range(5)]

    def column(self, dx):
        x = lax.rem(self.me.x + (dx + NX), NX)
        return self.buf.at[self.me.c, pl.ds(x * NYH, NYH)]

    def begin(self):
        me = self.me
        ref = self.buf.at[me.c, me.chip()]
        for dy in (1, -1, 2):
            self.wire.send(ref, ref, me.device(dy=dy), self.sent, self.in_y)

    def columns(self):
        me = self.me
        self.wire.take(self.in_y, self.buf.at[0, pl.ds(0, NYH - 1)])
        ref = self.column(0)
        for dx in (1, -1, 2):
            self.wire.send(ref, ref, me.device(dx=dx), self.sent, self.in_x)

    def pair(self):
        me = self.me
        self.wire.take(self.in_x, self.buf.at[0, pl.ds(0, (NX - 1) * NYH)])
        ref = self.buf.at[me.c]
        self.wire.send(ref, ref, me.device(dc=1), self.sib_out, self.sib)

    def end(self):
        self.wire.take(self.sib, self.buf.at[0])

    def finish(self):
        self.wire.take(self.sent, self.buf.at[0, pl.ds(0, NYH - 1 + (NX - 1) * NYH)])
        self.wire.take(self.sib_out, self.buf.at[0])


def add_into(dst, *others):
    total = dst[...].astype(jnp.float32)
    for other in others:
        total = total + other[...].astype(jnp.float32)
    dst[...] = total.astype(dst.dtype)


class TermScatter:
    def __init__(self, me, wire, terms, bufs):
        self.me, self.wire, self.terms = me, wire, terms
        (self.pair, self.part, self.far_up, self.far_down, self.near_up, self.near_down,
         self.row, self.yfar_up, self.yfar_down, self.ynear_up, self.ynear_down) = bufs
        new = wire.new
        self.pair_out, self.x_out, self.y_out = new(), new(), new()
        self.pair_in = {dx: new() for dx in (2, 1, -1, 0)}
        self.x_in, self.y_in = [new() for _ in range(6)], [new() for _ in range(6)]

    def at_x(self, dx):
        return lax.rem(self.me.x + (dx + NX), NX) * NYH

    def group(self, dx, first=0, count=NYH):
        return self.part.at[pl.ds(self.at_x(dx) + first, count)]

    def send_pair(self, dx):
        chips = pl.ds(self.at_x(dx), NYH)
        self.wire.send(
            self.terms.at[chips, 1 - self.me.c], self.pair.at[chips],
            self.me.device(dc=1), self.pair_out, self.pair_in[dx],
        )

    def add_pair(self, dx):
        first = self.at_x(dx)
        self.wire.take(self.pair_in[dx], self.pair.at[pl.ds(first, NYH)])
        for j in range(NYH):
            i = first + j
            self.part[i] = (
                self.terms[i, self.me.c].astype(jnp.float32) + self.pair[i].astype(jnp.float32)
            ).astype(jnp.bfloat16)

    def send_x(self, src, dst, k, dx):
        self.wire.send(src, dst, self.me.device(dx=dx), self.x_out, self.x_in[k])

    def x_start(self):
        half = NYH // 2
        self.send_x(self.group(2, 0, half), self.far_up, 0, 1)
        self.send_x(self.group(2, half, half), self.far_down, 1, -1)

    def x_up(self):
        half = NYH // 2
        self.send_x(self.group(1, half, half), self.near_up.at[pl.ds(half, half)], 2, 1)

    def x_down(self):
        half = NYH // 2
        self.send_x(self.group(-1, 0, half), self.near_down.at[pl.ds(0, half)], 3, -1)

    def x_far(self):
        half = NYH // 2
        self.wire.take(self.x_in[0], self.far_up)
        add_into(self.group(1, 0, half), self.far_up)
        self.send_x(self.group(1, 0, half), self.near_up.at[pl.ds(0, half)], 4, 1)
        self.wire.take(self.x_in[1], self.far_down)
        add_into(self.group(-1, half, half), self.far_down)
        self.send_x(self.group(-1, half, half), self.near_down.at[pl.ds(half, half)], 5, -1)

    def at_y(self, dy):
        return lax.rem(self.me.yh + (dy + NYH), NYH)

    def send_y(self, src, dst, k, dy):
        self.wire.send(src, dst, self.me.device(dy=dy), self.y_out, self.y_in[k])

    def along_y(self):
        half = NYH // 2
        for k, ref in ((2, self.near_up), (3, self.near_down), (4, self.near_up), (5, self.near_down)):
            self.wire.take(self.x_in[k], ref.at[pl.ds(0, half)])
        mine = self.at_x(0)
        row = self.row
        for i in range(NYH):
            row[i] = (
                self.part[mine + i].astype(jnp.float32)
                + self.near_up[i].astype(jnp.float32)
                + self.near_down[i].astype(jnp.float32)
            ).astype(jnp.bfloat16)
        rows = TOK // 2
        low, high = pl.ds(0, rows), pl.ds(rows, rows)
        at_y = self.at_y
        self.send_y(row.at[at_y(2), low], self.yfar_up, 0, 1)
        self.send_y(row.at[at_y(2), high], self.yfar_down, 1, -1)
        self.send_y(row.at[at_y(1), high], self.ynear_up.at[high], 2, 1)
        self.send_y(row.at[at_y(-1), low], self.ynear_down.at[low], 3, -1)

    def y_far(self):
        row, at_y = self.row, self.at_y
        rows = TOK // 2
        low, high = pl.ds(0, rows), pl.ds(rows, rows)
        self.wire.take(self.y_in[0], self.yfar_up)
        add_into(row.at[at_y(1), low], self.yfar_up)
        self.send_y(row.at[at_y(1), low], self.ynear_up.at[low], 4, 1)
        self.wire.take(self.y_in[1], self.yfar_down)
        add_into(row.at[at_y(-1), high], self.yfar_down)
        self.send_y(row.at[at_y(-1), high], self.ynear_down.at[high], 5, -1)

    def result(self):
        rows = TOK // 2
        low, high = pl.ds(0, rows), pl.ds(rows, rows)
        self.wire.take(self.y_in[2], self.ynear_up.at[high])
        self.wire.take(self.y_in[3], self.ynear_down.at[low])
        self.wire.take(self.y_in[4], self.ynear_up.at[low])
        self.wire.take(self.y_in[5], self.ynear_down.at[high])
        return (
            self.row[self.at_y(0)].astype(jnp.float32)
            + self.ynear_up[...].astype(jnp.float32)
            + self.ynear_down[...].astype(jnp.float32)
        )

    def finish(self):
        self.wire.take(self.pair_out, self.pair)
        self.wire.take(self.x_out, self.part.at[pl.ds(0, NX * NYH - NYH)])
        self.wire.take(self.y_out, self.row.at[pl.ds(0, NYH - 1)])


def dot(a, b, dims):
    return lax.dot_general(a, b, (dims, ((), ())), preferred_element_type=jnp.float32)


NN = ((1,), (0,))
NT = ((1,), (1,))
TN = ((0,), (0,))
F32, B16 = jnp.float32, jnp.bfloat16
SCALE = HD ** (-0.5)
ENC = (R / D) ** 0.5


def row_sum(values):
    return jnp.sum(values, axis=-1, keepdims=True)


def rms_of(total):
    return lax.rsqrt(total * (1.0 / D) + EPS)


def stack_heads(matrix):
    return jnp.concatenate([matrix[:, h * HD : (h + 1) * HD] for h in range(HQ)], axis=0)


def from_columns(columns):
    return jnp.concatenate(
        [columns[:, h * TOK : (h + 1) * TOK].T for h in range(HQ)], axis=1
    )


def to_columns(matrix):
    return jnp.concatenate([matrix[:, h * HD : (h + 1) * HD].T for h in range(HQ)], axis=1)


def tick_kernel(
    codes_ref, saved_ref, grads_ref, docs_f_ref, docs_b_ref, codec_ref, wqkv_ref, wout_ref,
    g1_ref, g2_ref,
    codes_out, grads_out,
    wk, wo, cd, meta, rows, sv, nb, st, gm, mx, kvf, kvb, probs, terms, codes, grads, sent, gin,
    both, other, tile,
    pair, part, far_up, far_down, near_up, near_down, row, yfar_up, yfar_down, ynear_up, ynear_down,
    sems, local_sems,
):
    me = Place()
    wire = Wire(sems)
    first = SectionGather(me, wire, wk, TOK)
    second = SectionGather(me, wire, wo, TOK)
    codec = CodecGather(me, wire, cd, both, other, tile)
    metas = MetaGather(me, wire, meta)
    back = SectionGather(me, wire, kvb, TOK)
    fore = SectionGather(me, wire, kvf, TOK)
    scatter = TermScatter(
        me, wire, terms,
        (pair, part, far_up, far_down, near_up, near_down, row,
         yfar_up, yfar_down, ynear_up, ynear_down),
    )
    codes_sent, codes_in, grads_sent, grads_in = [wire.new() for _ in range(4)]
    own = me.slot()
    sections = NYL * NZ
    after = {"section": lax.rem(me.section + 1, sections), "seq": me.seq}
    before = {"section": lax.rem(me.section + sections - 1, sections), "seq": me.seq}
    everyone = (0, -1, 1, 2)

    fills = []

    def fill(src, dst):
        copy = pltpu.make_async_copy(src, dst, local_sems.at[len(fills)])
        copy.start()
        fills.append(copy)
        return copy

    fill_k = fill(wqkv_ref.at[0, :, pl.ds(QW, 2 * HD)], wk.at[own])
    fill_w = [
        fill(wqkv_ref.at[0, :, pl.ds(0, QW)], wo.at[own, :, pl.ds(0, QW)]),
        fill(wout_ref.at[0], wo.at[own, :, pl.ds(QW, QW)]),
    ]
    fill_x = [fill(saved_ref.at[:, pl.ds(g * GW, GW)], sv.at[g]) for g in range(NG)]
    fill_x += [fill(codes_ref, codes), fill(grads_ref, grads)]
    tall = codec_ref[...].astype(F32)
    both[...] = jnp.concatenate([tall, tall], axis=0).astype(B16)
    docs_f, docs_b = docs_f_ref[...].astype(F32), docs_b_ref[...].astype(F32)
    meta[me.c, me.chip()] = jnp.concatenate(
        [docs_f, docs_b, g1_ref[...].astype(F32), g2_ref[...].astype(F32), jnp.zeros((4, TOK), F32)],
        axis=0,
    )
    meet(first.partners() + codec.partners() + [after, before])
    fill_k.wait()
    first.begin()
    codec.begin()
    metas.begin()
    for copy in fill_w:
        copy.wait()
    second.begin_x()
    for copy in fill_x:
        copy.wait()

    def square_step(g, total):
        values = sv[g].astype(F32)
        return total + row_sum(values * values)

    zero = jnp.zeros((TOK, 1), F32)
    codec.pair(local_sems.at[len(fills)])
    r1b = rms_of(lax.fori_loop(0, NG, square_step, zero))
    metas.columns()
    first.x_near(0)
    first.y_near()
    second.begin_y()
    codec.columns()
    second.x_near(0)
    metas.pair()
    first.y_far()
    first.x_near(-1)
    first.x_near(1)
    codec.planes()
    metas.end()
    for q in range(NSEQ):
        rows[q // GS, :, q % GS * TOK : (q % GS + 1) * TOK] = meta[q % NC, q // NC]

    def g1(g):
        return rows[g, 2:3, :]

    def g2(g):
        return rows[g, 3:4, :]

    @pl.loop(0, NG)
    def _(g):
        nb[g] = (sv[g].astype(F32) * r1b * g1(g)).astype(B16)

    first.x_far(0)
    first.x_near(2)
    second.y_near()
    first.x_far(-1, 1, 2)
    first.end()

    def wk_of(g):
        return wk[pl.ds(g * GS, GS)].reshape(GW, 2 * HD)

    def wq_of(g):
        return wo[pl.ds(g * GS, GS), :, :QW].reshape(GW, QW)

    def wo_of(g):
        return wo[pl.ds(g * GS, GS), :, QW:].reshape(GW, QW)

    def cd_of(g):
        return cd[pl.ds(pl.multiple_of(g * GW, GW), GW), :]

    def project(values, weights_of):
        def step(g, total):
            return total + dot(values[g], weights_of(g), NN)

        return lax.fori_loop(0, NG, step, jnp.zeros((TOK, QW), F32)).astype(B16)

    kvb[own] = project(nb, wk_of)
    back.begin()
    second.y_far()
    second.x_near(-1)
    second.x_near(1)
    codec.step(1)
    back.x_near(0)
    back.y_near()
    second.x_near(2)
    codec.step(2)
    back.y_far()
    second.x_far(*everyone)
    back.x_near(-1)
    back.x_near(1)
    codec.step(3)
    back.x_near(2)
    second.end()
    q_b = stack_heads(project(nb, wq_of))
    back.x_far(*everyone)
    codec.step(4)
    codec.end()

    def decode(g, total):
        wide = dot(jnp.concatenate([codes[...], grads[...]], axis=0), cd_of(g), NT)
        stream = wide[:TOK]
        st[g] = stream
        gm[g] = wide[TOK:] * ENC * g2(g)
        return total + row_sum(stream * stream)

    r1f = rms_of(lax.fori_loop(0, NG, decode, zero))

    @pl.loop(0, NG)
    def _(g):
        nb[g] = (st[g] * r1f * g1(g)).astype(B16)

    kvf[own] = project(nb, wk_of)
    fore.begin()
    back.end()

    q_pos = (own * TOK + lax.broadcasted_iota(jnp.int32, (1, TOK), 1)).astype(F32)
    q_pos = jnp.concatenate([q_pos] * HQ, axis=1)

    def starts(docs, index):
        zeros = D - jnp.sum(rows[:, index : index + 1, :], axis=(0, 2), keepdims=True)[0]
        return jnp.concatenate([docs * zeros] * HQ, axis=1)

    def keys_of(kv, i):
        return kv[pl.ds(i * KS, KS), :, :HD].reshape(KEYS, HD)

    def values_of(kv, i):
        return kv[pl.ds(i * KS, KS), :, HD:].reshape(KEYS, HD)

    def tops(kv, queries, start):
        def step(i, top):
            scores = dot(keys_of(kv, i), queries, NT) * SCALE
            k_pos = (
                i * KEYS + lax.broadcasted_iota(jnp.int32, (KEYS, HQ * TOK), 0)
            ).astype(F32)
            scores = jnp.where((k_pos >= start) & (k_pos <= q_pos), scores, -1e30)
            probs[i] = scores
            return jnp.maximum(top, jnp.max(scores, axis=0, keepdims=True))

        return lax.fori_loop(0, NK, step, jnp.full((1, HQ * TOK), -1e30, F32))

    def attended(kv, top):
        def step(i, carry):
            total, accum = carry
            p = jnp.exp(probs[i] - top)
            probs[i] = p
            total = total + jnp.sum(p, axis=0, keepdims=True)
            return total, accum + dot(values_of(kv, i), p.astype(B16), TN)

        total, accum = lax.fori_loop(
            0, NK, step, (jnp.zeros((1, HQ * TOK), F32), jnp.zeros((HD, HQ * TOK), F32))
        )
        return total, (accum / total).astype(B16)

    top = tops(kvb, q_b, starts(docs_b, 1))
    denom, att_cols = attended(kvb, top)
    att_cols = att_cols.astype(F32)
    att = from_columns(att_cols).astype(B16)

    fore.x_near(0)
    fore.y_near()

    def mix_b(g, carry):
        squares, cross = carry
        mixed = sv[g].astype(F32) + dot(att, wo_of(g), NT)
        mx[g] = mixed
        return squares + row_sum(mixed * mixed), cross + row_sum(mixed * gm[g])

    squares, cross = lax.fori_loop(0, NG, mix_b, (zero, zero))
    r2b = rms_of(squares)
    lean = r2b * r2b * cross * (1.0 / D)
    fore.y_far()

    def grad_mix(g, total):
        grad = r2b * (gm[g] - mx[g] * lean)
        gm[g] = grad
        return total + dot(grad.astype(B16), wo_of(g), NN)

    grad_att = lax.fori_loop(0, NG, grad_mix, jnp.zeros((TOK, QW), F32)).astype(B16)
    g_heads = stack_heads(grad_att)
    delta = jnp.sum(to_columns(grad_att.astype(F32)) * att_cols, axis=0, keepdims=True)
    inverse = 1.0 / denom

    def backward_step(i, total):
        p = probs[i] * inverse
        grad_p = dot(values_of(kvb, i), g_heads, NT)
        grad_s = (p * (grad_p - delta) * SCALE).astype(B16)
        chips = pl.ds(i * (KS // NC), KS // NC)
        shape = (KS // NC, NC, TOK, HD)
        terms[chips, :, :, :HD] = dot(grad_s, q_b, NN).astype(B16).reshape(shape)
        terms[chips, :, :, HD:] = dot(p.astype(B16), g_heads, NN).astype(B16).reshape(shape)
        return total + dot(keys_of(kvb, i), grad_s, TN)

    grad_q = jnp.zeros((HD, HQ * TOK), F32)
    per = NK // NG

    def backward(dx, total):
        g = lax.rem(me.x + (dx + NX), NX)
        total = lax.fori_loop(g * per, (g + 1) * per, backward_step, total)
        scatter.send_pair(dx)
        return total

    grad_q = backward(2, grad_q)
    fore.x_near(-1)
    grad_q = backward(1, grad_q)
    scatter.add_pair(2)
    scatter.x_start()
    fore.x_near(1)
    grad_q = backward(-1, grad_q)
    scatter.add_pair(1)
    scatter.x_up()
    fore.x_near(2)
    grad_q = backward(0, grad_q)
    scatter.add_pair(-1)
    scatter.x_down()
    scatter.x_far()
    fore.x_far(*everyone)
    scatter.add_pair(0)
    grad_q = from_columns(grad_q).astype(B16)
    q_f = stack_heads(project(nb, wq_of))
    fore.end()

    top = tops(kvf, q_f, starts(docs_f, 0))
    scatter.along_y()
    _, att_cols = attended(kvf, top)
    att = from_columns(att_cols.astype(F32)).astype(B16)
    scatter.y_far()

    def mix_f(g, total):
        mixed = st[g] + dot(att, wo_of(g), NT)
        st[g] = mixed
        return total + row_sum(mixed * mixed)

    r2f = rms_of(lax.fori_loop(0, NG, mix_f, zero))

    def encode(g, total):
        normed = (st[g] * r2f * g2(g)).astype(B16)
        return total + dot(normed, cd_of(g), NN)

    coded = lax.fori_loop(0, NG, encode, jnp.zeros((TOK, R), F32))
    sent[...] = (coded * ENC).astype(B16)
    wire.send(sent, codes_out, after, codes_sent, codes_in)

    kv_grad = scatter.result().astype(B16)

    def grad_norm(g, total):
        weighted = (dot(grad_q, wq_of(g), NT) + dot(kv_grad, wk_of(g), NT)) * g1(g)
        mx[g] = weighted
        return total + row_sum(weighted * sv[g].astype(F32))

    cross = lax.fori_loop(0, NG, grad_norm, zero)
    lean1 = r1b * r1b * cross * (1.0 / D)

    def grad_code(g, total):
        grad = gm[g] + r1b * (mx[g] - sv[g].astype(F32) * lean1)
        return total + dot(grad.astype(B16), cd_of(g), NN)

    gin[...] = lax.fori_loop(0, NG, grad_code, jnp.zeros((TOK, R), F32)).astype(B16)
    wire.send(gin, grads_out, before, grads_sent, grads_in)
    for gather in (first, second, codec, metas, back, fore, scatter):
        gather.finish()
    wire.take(codes_sent, sent)
    wire.take(codes_in, codes_out)
    wire.take(grads_sent, gin)
    wire.take(grads_in, grads_out)


ANY = pl.BlockSpec(memory_space=pl.ANY)
VMEM = pl.BlockSpec(memory_space=pltpu.VMEM)


def on_device(
    codes_fwd, saved_stream, grad_codes, docs_fwd, docs_bwd, codec, wqkv, wout, gain_attn, gain_code
):
    half = NYH // 2
    codes, grads = pl.pallas_call(
        tick_kernel,
        out_shape=(jax.ShapeDtypeStruct((TOK, R), B16),) * 2,
        in_specs=[ANY, ANY, ANY, VMEM, VMEM, VMEM, ANY, ANY, VMEM, VMEM],
        out_specs=(VMEM, VMEM),
        scratch_shapes=[
            pltpu.VMEM((NSEQ, TOK, 2 * HD), B16),
            pltpu.VMEM((NSEQ, TOK, 2 * QW), B16),
            pltpu.VMEM((D, R), B16),
            pltpu.VMEM((NC, NX * NYH, 8, TOK), F32),
            pltpu.VMEM((NG, 8, GW), F32),
            pltpu.VMEM((NG, TOK, GW), B16),
            pltpu.VMEM((NG, TOK, GW), B16),
            pltpu.VMEM((NG, TOK, GW), F32),
            pltpu.VMEM((NG, TOK, GW), F32),
            pltpu.VMEM((NG, TOK, GW), F32),
            pltpu.VMEM((NSEQ, TOK, 2 * HD), B16),
            pltpu.VMEM((NSEQ, TOK, 2 * HD), B16),
            pltpu.VMEM((NK, KEYS, HQ * TOK), F32),
            pltpu.VMEM((NX * NYH, NC, TOK, 2 * HD), B16),
            pltpu.VMEM((TOK, R), B16),
            pltpu.VMEM((TOK, R), B16),
            pltpu.VMEM((TOK, R), B16),
            pltpu.VMEM((TOK, R), B16),
            pltpu.VMEM((CROWS, R), B16),
            pltpu.VMEM((CROWS, R), B16),
            pltpu.VMEM((CROWS, R), B16),
            pltpu.VMEM((NX * NYH, TOK, 2 * HD), B16),
            pltpu.VMEM((NX * NYH, TOK, 2 * HD), B16),
            pltpu.VMEM((half, TOK, 2 * HD), B16),
            pltpu.VMEM((half, TOK, 2 * HD), B16),
            pltpu.VMEM((NYH, TOK, 2 * HD), B16),
            pltpu.VMEM((NYH, TOK, 2 * HD), B16),
            pltpu.VMEM((NYH, TOK, 2 * HD), B16),
            pltpu.VMEM((TOK // 2, 2 * HD), B16),
            pltpu.VMEM((TOK // 2, 2 * HD), B16),
            pltpu.VMEM((TOK, 2 * HD), B16),
            pltpu.VMEM((TOK, 2 * HD), B16),
            pltpu.SemaphoreType.DMA((SEMAPHORES,)),
            pltpu.SemaphoreType.DMA((10,)),
        ],
        compiler_params=pltpu.CompilerParams(
            collective_id=0, has_side_effects=True, vmem_limit_bytes=56 * 2**20
        ),
        name="tick",
    )(
        codes_fwd[0], saved_stream[0], grad_codes[0], docs_fwd, docs_bwd, codec, wqkv, wout,
        gain_attn, gain_code,
    )
    return codes[None], grads[None]


def solution(mesh):
    return jax.shard_map(
        on_device,
        mesh=mesh,
        in_specs=(
            P("section", "seq", None),
            P("section", "seq", None),
            P("section", "seq", None),
            P("section", "seq"),
            P("section", "seq"),
            P(("section", "seq"), None),
            P("section", "seq", None),
            P("section", "seq", None),
            P("section", "seq"),
            P("section", "seq"),
        ),
        out_specs=(P("section", "seq", None), P("section", "seq", None)),
        check_vma=False,
    )
```
